32 devices in a mesh: rep: 4 (over y, x), exp: 8 (over z, core).
Axes of the slice: x: 2, y: 2, z: 4, core: 2. Of those that a mesh axis runs over, the one named last changes fastest.
Arguments:
- tokens: bfloat16 [2048, 1024], P('exp', 'rep'), may hold values from -6 to 6
- routes: int32 [2048, 2], P('exp'), may hold values from 0 to 7, all different within a row; in each aligned block of 256 rows (0 to 255, 256 to 511, ...) at most 128 rows name the same one
- probs: float32 [2048, 2], P('exp'), may hold values from 0.2 to 1
- capacity: int32 [8], replicated, may hold values from 256 to 767
- plan: int32 [8], replicated, may hold values from 0 to 7, each once
- grad_out: bfloat16 [2048, 1024], P('exp', 'rep'), may hold values from -6 to 6
- w_gate: bfloat16 [8, 1024, 4096], P('exp', None, 'rep'), may hold values from -0.1875 to 0.1875
- w_up: bfloat16 [8, 1024, 4096], P('exp', None, 'rep'), may hold values from -0.1875 to 0.1875
- w_down: bfloat16 [8, 4096, 1024], P('exp', 'rep'), may hold values from -0.09375 to 0.09375
Outputs:
- mixed: bfloat16 [2048, 1024], P('exp', 'rep')
- grad_tokens: bfloat16 [2048, 1024], P('exp', 'rep')
- grad_probs: float32 [2048, 2], P('exp')
- grad_gate: float32 [8, 1024, 4096], P('exp', None, 'rep')
- grad_up: float32 [8, 1024, 4096], P('exp', None, 'rep')
- grad_down: float32 [8, 4096, 1024], P('exp', 'rep')
The draws below stay inside these ranges and needn't reach their ends.
Inputs may be any that keep to these rules, and one draw needn't show every extreme that they name: `routes`: each row names two different experts; among the rows of one block of 256 tokens no expert is named more than 128 times, a bound that some block reaches. `plan`: a permutation of the experts; its first 4 entries are the hot experts.
All inputs are finite; a program needn't handle non-finite values.
Results may differ from the reference program's by a relative error of at most 0.01.
Values may be sent and summed in bfloat16 or wider, within the bound.
No kernel may reach another device: no remote copies, remote signals or barrier semaphores. Data moves between devices by JAX's collectives and lax.ppermute only.
A program may use at most 128 MiB of HBM per device.

```python
import math
import jax
import jax.numpy as jnp
import numpy as np
from jax import lax

D = 1024
FF = 4096
TOK_DEV = 256
HOT = 4
EXPERTS = 8
TOKENS = 2048
PER = 128
SHADOW = 512
N_REP = 4
N_EXP = 8


def set_ends(result, own_key, least, high):
    index_at = [jax.random.randint(jax.random.fold_in(own_key, axis), (), 0, length) for axis, length in enumerate(result.shape)]
    main_axis = result.shape.index(max(result.shape))
    beside = index_at[:main_axis] + [(index_at[main_axis] + 1) % result.shape[main_axis]] + index_at[main_axis + 1:]
    return result.at[tuple(index_at)].set(least).at[tuple(beside)].set(high)


def shard_levels(stream_key, extent, shards, low, largest):
    gain = 1.0
    for axis_at, shards_of in shards:
        heights = jax.random.uniform(jax.random.fold_in(jax.random.fold_in(stream_key, 6), axis_at), (shards_of,), jnp.float32, low / len(shards), largest / len(shards))
        gain = gain * jnp.repeat(jnp.exp(heights), extent[axis_at] // shards_of).reshape((-1,) + (1,) * (len(extent) - 1 - axis_at))
    return gain


def deal_out(own_key, own, number, rows, count, top, most, skew):
    sequence = jax.random.permutation(own_key, count)
    heavy_load, common = load_shares(count, rows * top, most, skew, True), load_shares(count, rows * top, most, skew, False)
    places = jnp.arange(count)

    def named(tallies, turn):
        used = int((tallies > 0).sum())
        fixed = max(1, used // 4)
        passed = fixed + (places - fixed + turn * (used - fixed)) % max(1, count - fixed)
        return jnp.zeros((count,), jnp.int32).at[sequence[jnp.where(places < fixed, places, passed)]].set(jnp.asarray(tallies, jnp.int32))

    tallies = jnp.where(number % 4 == 0, named(heavy_load, number // 4), named(common, number - number // 4 - 1))
    mixed = jax.random.permutation(jax.random.fold_in(own, 3), count)
    source_of, taker = mixed[0:count // 2 * 2:2], mixed[1:count // 2 * 2:2]
    room = jnp.minimum(tallies[source_of] - 1, most - tallies[taker]) // 2
    room = jnp.where((source_of == sequence[0]) | (taker == sequence[0]) | (tallies[taker] == 0), 0, jnp.maximum(room, 0))
    passed = jax.random.randint(jax.random.fold_in(own, 4), (count // 2,), 0, 1 << 20) % (room + 1)
    tallies = tallies.at[source_of].add(-passed).at[taker].add(passed)
    items = jnp.searchsorted(jnp.cumsum(tallies), jnp.arange(rows * top), side="right").astype(jnp.int32)
    grid = items.reshape(top, rows).T
    grid = grid[jax.random.permutation(jax.random.fold_in(own, 1), rows)]
    turn = jax.random.randint(jax.random.fold_in(own, 2), (rows, 1), 0, top)
    return jnp.take_along_axis(grid, (jnp.arange(top)[None, :] + turn) % top, axis=1)


def load_shares(count, total, most, lean, full):
    weights = [(1 << 20) // math.isqrt(standing ** lean) + 1 for standing in range(1, count + 1)]
    largest = most if full else min(most, max(-(-total // count), total * weights[0] // sum(weights)))
    least = 1 if total - largest >= count - 1 else 0
    given, spare = [largest] + [least] * (count - 1), total - largest - least * (count - 1)
    while spare > 0:
        movable = [i for i in range(1, count) if given[i] < largest] or [i for i in range(1, count) if given[i] < most]
        pool, budget = sum([weights[i] for i in movable]), spare
        for i in movable:
            more = min(most - given[i], max(1, budget * weights[i] // pool), spare)
            given[i] = given[i] + more
            spare = spare - more
    return np.array(given)


def gaussian(own_key, extent, spread, most, pieces=(), kind=jnp.bfloat16):
    drawn = spread * jax.random.normal(own_key, extent, jnp.float32)
    if pieces:
        drawn = drawn * shard_levels(own_key, extent, pieces, -0.22, 0.18)
    return jnp.clip(drawn, -most, most).astype(kind)


def setup_inputs(seed: int = 0) -> dict:
    splits = jax.random.split(jax.random.key(seed), 10)
    tokens = gaussian(splits[0], (TOKENS, D), 1.0, 6.0, ((0, 8), (1, 4)))
    routes_keys = jax.random.split(jax.random.fold_in(splits[1], 1), TOKENS // TOK_DEV)
    routes_turns = jax.random.permutation(jax.random.fold_in(splits[1], 3), TOKENS // TOK_DEV)
    routes = jax.vmap(lambda own, number: deal_out(jax.random.fold_in(splits[1], 2), own, number, TOK_DEV, EXPERTS, 2, PER, 2))(routes_keys, routes_turns).reshape((TOKENS, 2))
    probs = jnp.clip(0.2 + 0.8 * jax.random.uniform(splits[2], (TOKENS, 2), jnp.float32) ** shard_levels(splits[2], (TOKENS, 2), ((0, 8),), -0.2, 0.2), 0.2, 1.0)
    capacity = set_ends(jax.random.randint(splits[3], (EXPERTS,), TOK_DEV, 3 * TOK_DEV), jax.random.fold_in(splits[3], 1), TOK_DEV, (3 * TOK_DEV) - 1).astype(jnp.int32)
    plan = jax.random.permutation(splits[4], EXPERTS).astype(jnp.int32)
    grad_out = gaussian(splits[5], (TOKENS, D), 1.0, 6.0, ((0, 8), (1, 4)))
    w_gate = gaussian(splits[6], (EXPERTS, D, FF), D ** -0.5, 0.1875, ((0, 8), (2, 4)))
    w_up = gaussian(splits[7], (EXPERTS, D, FF), D ** -0.5, 0.1875, ((0, 8), (2, 4)))
    w_down = gaussian(splits[8], (EXPERTS, FF, D), FF ** -0.5, 0.09375, ((0, 8), (1, 4)))
    return dict(tokens=tokens, routes=routes, probs=probs, capacity=capacity, plan=plan, grad_out=grad_out, w_gate=w_gate, w_up=w_up, w_down=w_down)


def reference(tokens, routes, probs, capacity, plan, grad_out, w_gate, w_up, w_down):
    flat = routes.reshape(-1).astype(jnp.int32)
    expert_ids = jnp.arange(EXPERTS, dtype=jnp.int32)
    onehot = (flat[:, None] == expert_ids[None, :]).astype(jnp.int32)
    position = jnp.sum((jnp.cumsum(onehot, axis=0).astype(jnp.int32) - onehot) * onehot, axis=1).astype(jnp.int32)
    blocks = onehot.reshape(N_EXP, 2 * TOK_DEV, EXPERTS)
    local_rank = jnp.sum((jnp.cumsum(blocks, axis=1).astype(jnp.int32) - blocks) * blocks, axis=2).reshape(-1).astype(jnp.int32)
    hot_flag = jnp.any(plan[:HOT][:, None] == expert_ids[None, :], axis=0).astype(jnp.int32)
    limit = capacity + SHADOW * hot_flag
    keep = (position < jnp.sum(onehot * limit[None, :], axis=1)).astype(jnp.float32)
    weight = probs.reshape(-1) * keep
    token_of = (jnp.arange(2 * TOKENS, dtype=jnp.int32) // 2).astype(jnp.int32)
    slot = ((token_of // TOK_DEV) * PER + local_rank).astype(jnp.int32)
    slots = N_EXP * PER
    group = FF // N_REP
    inputs_rows = jnp.zeros((EXPERTS, slots, D), jnp.bfloat16).at[flat, slot].set(tokens[token_of])
    scaled = (weight[:, None] * grad_out[token_of].astype(jnp.float32)).astype(jnp.bfloat16)
    grads_rows = jnp.zeros((EXPERTS, slots, D), jnp.bfloat16).at[flat, slot].set(scaled)

    def grouped(left, right):
        left_parts = left.reshape(slots, N_REP, group).transpose(1, 0, 2).astype(jnp.float32)
        return jnp.einsum("nrf,nfd->nrd", left_parts, right.reshape(N_REP, group, D).astype(jnp.float32))

    def one_expert(operands):
        xs, dout, wg, wu, wd = operands
        gate = jnp.dot(xs, wg, preferred_element_type=jnp.float32)
        up = jnp.dot(xs, wu, preferred_element_type=jnp.float32)
        sig = jax.nn.sigmoid(gate)
        silu = gate * sig
        hidden = (silu * up).astype(jnp.bfloat16)
        parts = lax.optimization_barrier(grouped(hidden, wd).astype(jnp.bfloat16))
        out = jnp.sum(parts.astype(jnp.float32), axis=0).astype(jnp.bfloat16)
        dh = jnp.dot(dout, wd.T, preferred_element_type=jnp.float32)
        dgate = (dh * up * sig * (1.0 + gate * (1.0 - sig))).astype(jnp.bfloat16)
        dup = (dh * silu).astype(jnp.bfloat16)
        gdown = jnp.dot(hidden.T, dout, preferred_element_type=jnp.float32)
        ggate = jnp.dot(xs.T, dgate, preferred_element_type=jnp.float32)
        gup = jnp.dot(xs.T, dup, preferred_element_type=jnp.float32)
        dparts = grouped(dgate, wg.T) + grouped(dup, wu.T)
        dparts = lax.optimization_barrier(dparts.astype(jnp.bfloat16))
        dxs = jnp.sum(dparts.astype(jnp.float32), axis=0).astype(jnp.bfloat16)
        return out, dxs, ggate, gup, gdown

    outs, dxs, grad_gate, grad_up, grad_down = lax.map(one_expert, (inputs_rows, grads_rows, w_gate, w_up, w_down))
    picked = outs[flat, slot].astype(jnp.float32)
    mixed = jnp.sum((weight[:, None] * picked).reshape(TOKENS, 2, D), axis=1).astype(jnp.bfloat16)
    dots = jnp.sum(grad_out[token_of].astype(jnp.float32) * picked, axis=1)
    grad_probs = (keep * dots).reshape(TOKENS, 2)
    back = dxs[flat, slot].astype(jnp.float32)
    grad_tokens = jnp.sum((weight[:, None] * back).reshape(TOKENS, 2, D), axis=1).astype(jnp.bfloat16)
    return mixed, grad_tokens, grad_probs, grad_gate, grad_up, grad_down
```

```python
import functools

import jax
import jax.numpy as jnp
from jax import lax
from jax.experimental import pallas as pl
from jax.experimental.pallas import tpu as pltpu
from jax.sharding import PartitionSpec as P

HOT = 4


def carried_in(value, axis, combine, identity):
    peers, mine = (lax.axis_size(axis), lax.axis_index(axis))
    everything = lax.all_gather(value, axis)
    start = jnp.broadcast_to(jnp.asarray(identity, value.dtype), value.shape)

    def step(k, before):
        reached = k < mine
        new = combine(before, everything[k])
        return jnp.where(reached, new, before)

    return lax.fori_loop(0, peers, step, start)


def fill_rows(shard, flat, rank, token_of, scale, experts, per_slot):
    picked = shard[token_of]
    if scale is not None:
        picked = (picked.astype(jnp.float32) * scale[:, None]).astype(jnp.bfloat16)
    empty = jnp.zeros((experts, per_slot, shard.shape[1]), jnp.bfloat16)
    return empty.at[flat, rank].set(picked)


def dispatch(shard, flat, rank, token_of, scale, experts, per_slot):
    buffer = fill_rows(shard, flat, rank, token_of, scale, experts, per_slot)
    received = lax.all_to_all(buffer, "exp", split_axis=0, concat_axis=0, tiled=True)
    narrow = received.reshape(-1, received.shape[2])
    return lax.all_gather(narrow, "rep", axis=1, tiled=True)


def return_rows(rows, flat, rank, experts, per_slot):
    back = lax.all_to_all(
        rows.reshape(experts, per_slot, rows.shape[1]),
        "exp",
        split_axis=0,
        concat_axis=0,
        tiled=True,
    )
    return back[flat, rank].astype(jnp.float32)


def on_device(tokens, routes, probs, capacity, plan, grad_out, w_gate, w_up, w_down):
    tok_rows = tokens.shape[0]
    experts = capacity.shape[0]
    per_slot = 4 * tok_rows // experts
    feat_cols = tokens.shape[1]
    flat = routes.reshape(-1)
    expert_ids = jnp.arange(experts, dtype=jnp.int32)
    onehot = (flat[:, None] == expert_ids[None, :]).astype(jnp.int32)
    rank = jnp.sum((jnp.cumsum(onehot, axis=0) - onehot) * onehot, axis=1)
    counts = jnp.sum(onehot, axis=0)
    earlier = carried_in(
        counts, "exp", lambda first, second: first + second, jnp.zeros_like(counts)
    )
    position = rank + jnp.sum(onehot * earlier[None, :], axis=1)
    hot_flag = jnp.any(plan[:HOT][:, None] == expert_ids[None, :], axis=0).astype(jnp.int32)
    limit = capacity + 2 * tok_rows * hot_flag
    keep = (position < jnp.sum(onehot * limit[None, :], axis=1)).astype(jnp.float32)
    weight = probs.reshape(-1) * keep
    token_of = jnp.arange(2 * tok_rows, dtype=jnp.int32) // 2
    wg = w_gate[0]
    wu = w_up[0]
    wd = w_down[0]
    xs = dispatch(tokens, flat, rank, token_of, None, experts, per_slot)
    gate = jnp.dot(xs, wg, preferred_element_type=jnp.float32)
    up = jnp.dot(xs, wu, preferred_element_type=jnp.float32)
    sig = jax.nn.sigmoid(gate)
    silu = gate * sig
    hidden = (silu * up).astype(jnp.bfloat16)
    partial_value = jnp.dot(hidden, wd, preferred_element_type=jnp.float32)
    out_rows = lax.psum_scatter(
        partial_value.astype(jnp.bfloat16), "rep", scatter_dimension=1, tiled=True
    )
    picked = return_rows(out_rows, flat, rank, experts, per_slot)
    mixed = jnp.sum((weight[:, None] * picked).reshape(tok_rows, 2, feat_cols), axis=1).astype(
        jnp.bfloat16
    )
    dots = jnp.sum(grad_out[token_of].astype(jnp.float32) * picked, axis=1)
    dots = lax.psum(dots, "rep")
    grad_probs = (keep * dots).reshape(tok_rows, 2)
    dout = dispatch(grad_out, flat, rank, token_of, weight, experts, per_slot)
    dh = lax.dot_general(dout, wd, (((1,), (1,)), ((), ())), preferred_element_type=jnp.float32)
    dgate = (dh * up * sig * (1.0 + gate * (1.0 - sig))).astype(jnp.bfloat16)
    dup = (dh * silu).astype(jnp.bfloat16)
    grad_down = lax.dot_general(
        hidden, dout, (((0,), (0,)), ((), ())), preferred_element_type=jnp.float32
    )
    grad_gate = lax.dot_general(
        xs, dgate, (((0,), (0,)), ((), ())), preferred_element_type=jnp.float32
    )
    grad_up = lax.dot_general(xs, dup, (((0,), (0,)), ((), ())), preferred_element_type=jnp.float32)
    dpartial = lax.dot_general(
        dgate, wg, (((1,), (1,)), ((), ())), preferred_element_type=jnp.float32
    )
    dpartial = dpartial + lax.dot_general(
        dup, wu, (((1,), (1,)), ((), ())), preferred_element_type=jnp.float32
    )
    dx_rows = lax.psum_scatter(
        dpartial.astype(jnp.bfloat16), "rep", scatter_dimension=1, tiled=True
    )
    back = return_rows(dx_rows, flat, rank, experts, per_slot)
    grad_tokens = jnp.sum((weight[:, None] * back).reshape(tok_rows, 2, feat_cols), axis=1).astype(
        jnp.bfloat16
    )
    return (mixed, grad_tokens, grad_probs, grad_gate[None], grad_up[None], grad_down[None])


F32 = jnp.float32
BF16 = jnp.bfloat16
I32 = jnp.int32
CHIPS = 4
VMEM_BYTES = 56 * 1024 * 1024


def dot(a, b, dims=((1,), (0,))):
    return lax.dot_general(a, b, (dims, ((), ())), preferred_element_type=F32)


def params(**kw):
    return pltpu.CompilerParams(vmem_limit_bytes=VMEM_BYTES, **kw)


def vmem():
    return pl.BlockSpec(memory_space=pltpu.VMEM)


def smem():
    return pl.BlockSpec(memory_space=pltpu.SMEM)


def place_rows(ids, own, par, per):
    z, c = ids[0], ids[1]
    toks = own.shape[1]
    row = lax.broadcasted_iota(I32, (2 * CHIPS, toks), 0)
    expert = 2 * (z ^ (row % CHIPS)) + c
    first = row < CHIPS
    named = [
        jnp.where(first, own[k : k + 1, :], par[k : k + 1, :]).astype(I32) == expert
        for k in range(2)
    ]
    either = jnp.logical_or(named[0], named[1])
    before = lax.broadcasted_iota(I32, (toks, toks), 0) < lax.broadcasted_iota(
        I32, (toks, toks), 1
    )
    rank = dot(either.astype(F32).astype(BF16), before.astype(F32).astype(BF16)).astype(I32)
    return row, expert, named, either, rank


def pick(rank, either, i, per):
    at = jnp.where(either[i : i + 1, :], rank[i : i + 1, :], -1)
    slots = lax.broadcasted_iota(I32, (per, at.shape[1]), 0)
    return (slots == at).astype(F32)


def x_kernel(per, ids, own_m, par_m, own_x, par_x, x0, x1, x2, x3):
    own, par = own_m[...], par_m[...]
    toks = own.shape[1]
    row, _, _, either, rank = place_rows(ids, own, par, per)
    place = either.astype(I32)
    tail = lax.broadcasted_iota(I32, (16, toks), 0)
    extra = jnp.zeros((16, toks), F32)
    for i, line in enumerate((own[0:1, :], own[1:2, :], par[0:1, :], par[1:2, :])):
        extra = jnp.where(tail == i, line, extra)
    for q, out in enumerate((x0, x1, x2, x3)):
        for src, ref in enumerate((own_x, par_x)):
            hot = pick(rank, place > 0, CHIPS * src + q, per).astype(BF16)
            out[src * per : (src + 1) * per, :] = dot(hot, ref[...]).astype(BF16)
        if q:
            out[2 * per : 2 * per + 16, :] = extra.astype(BF16)


def g_kernel(
    per, extra_slots, ids, cap, plan, own_m, par_m, e1, e2, e3, own_g, par_g, g0, g1, g2, g3, info
):
    own, par = own_m[...], par_m[...]
    toks = own.shape[1]
    z, c = ids[0], ids[1]
    row, expert, named, either, rank = place_rows(ids, own, par, per)
    expert_col = expert[:, 0:1]
    q_col = row[:, 0:1] % CHIPS
    first_col = row[:, 0:1] < CHIPS
    limit = jnp.zeros((2 * CHIPS, 1), I32)
    for q in range(CHIPS):
        e = 2 * (z ^ q) + c
        room = cap[e]
        for h in range(HOT):
            room = room + jnp.where(plan[h] == e, extra_slots, 0)
        limit = jnp.where(q_col == q, room, limit)
    earlier = jnp.zeros((2 * CHIPS, 1), F32)
    remote = (None, e1, e2, e3)
    for p in range(CHIPS):
        table = None if p == 0 else remote[p][...].astype(F32)
        for s in range(2):
            if p == 0:
                lines = [(own, par)[s][k : k + 1, :] for k in range(2)]
            else:
                lines = [table[2 * s + k : 2 * s + k + 1, :] for k in range(2)]
            hits = jnp.logical_or(
                lines[0].astype(I32) == expert, lines[1].astype(I32) == expert
            ).astype(F32)
            count = jnp.sum(hits, axis=1, keepdims=True)
            block = 2 * (z ^ p) + (c ^ s)
            ahead = jnp.where(
                first_col,
                (block < 2 * z + c).astype(F32),
                (block < 2 * z + (c ^ 1)).astype(F32),
            )
            earlier = earlier + count * ahead
    position = rank + earlier.astype(I32)
    keep = jnp.where(position < limit, 1.0, 0.0)
    first = row < CHIPS
    weight = jnp.zeros((2 * CHIPS, toks), F32)
    lines = []
    for k in range(2):
        prob = jnp.where(first, own[2 + k : 3 + k, :], par[2 + k : 3 + k, :])
        mine = named[k].astype(F32)
        weight = weight + mine * keep * prob
        lines.append((mine * (row % CHIPS * per + rank + 1).astype(F32), mine * keep * prob, mine * keep))
    at = lax.broadcasted_iota(I32, (128, toks), 0)
    table = jnp.zeros((128, toks), F32)
    for kind in range(3):
        for src in range(2):
            for k in range(2):
                line = jnp.sum(
                    jnp.where(first if src == 0 else jnp.logical_not(first), lines[k][kind], 0.0),
                    axis=0,
                    keepdims=True,
                )
                table = jnp.where(at == 4 * kind + 2 * src + k, line, table)
    info[...] = jnp.transpose(table)
    for q, out in enumerate((g0, g1, g2, g3)):
        for src, ref in enumerate((own_g, par_g)):
            i = CHIPS * src + q
            hot = pick(rank, either, i, per)
            scale = jnp.sum(hot * weight[i : i + 1, :], axis=1, keepdims=True)
            rows = dot(hot.astype(BF16), ref[...])
            out[src * per : (src + 1) * per, :] = (rows * scale).astype(BF16)


def combine(per, src, k, rows, info):
    slot = info[:, 2 * src + k : 2 * src + k + 1].astype(I32) - 1
    slots = lax.broadcasted_iota(I32, (info.shape[0], CHIPS * per), 1)
    return dot((slots == slot).astype(F32).astype(BF16), rows)


def back_kernel(per, with_dots, y0, y1, y2, y3, info_ref, *refs):
    if with_dots:
        own_g, par_g, kept, sent = refs
    else:
        kept, sent = refs
    info = info_ref[...]
    feats = y0.shape[1]
    toks = info.shape[0]
    lane = lax.broadcasted_iota(I32, (toks, 128), 1)
    for src, out in enumerate((kept, sent)):
        rows = jnp.concatenate([y[src * per : (src + 1) * per, :] for y in (y0, y1, y2, y3)], axis=0)
        total = jnp.zeros((toks, feats), F32)
        dots = jnp.zeros((toks, 128), F32)
        for k in range(2):
            picked = combine(per, src, k, rows, info)
            at = 2 * src + k
            total = total + info[:, 4 + at : 5 + at] * picked
            if with_dots:
                grad = (own_g, par_g)[src][...].astype(F32)
                inner = jnp.sum(grad * picked, axis=1, keepdims=True) * info[:, 8 + at : 9 + at]
                dots = jnp.where(lane == k, inner, dots)
        out[:, 0:feats] = total
        if with_dots:
            out[:, feats : feats + 128] = dots


def assemble(r, shards, cat):
    own, a, b, c, d = shards
    feats = own.shape[1]
    half = c.shape[0]

    def cols(k):
        return pl.ds(pl.multiple_of((r ^ k) * feats, feats), feats)

    cat[:, cols(0)] = own[...]
    cat[:, cols(1)] = a[...]
    cat[:, cols(2)] = b[...]
    cat[0:half, cols(3)] = c[...]
    cat[half : 2 * half, cols(3)] = d[...]


def split_out(r, total, feats, outs):
    send_a, keep_a, send_b, keep_b = outs
    half = send_a.shape[0]
    for rows, out, pair in (
        (0, send_a, (1, 3)),
        (0, keep_a, (0, 2)),
        (half, send_b, (2, 3)),
        (half, keep_b, (0, 1)),
    ):
        for n, k in enumerate(pair):
            cols = pl.ds(pl.multiple_of((r ^ k) * feats, feats), feats)
            out[:, n * feats : (n + 1) * feats] = total[rows : rows + half, cols].astype(BF16)


def forward_kernel(ids, own, a, b, c, d, wg, wu, wd, cat, hid, act, slope, sa, ka, sb, kb, total, gs, us):
    j = pl.program_id(0)
    r = ids[2]

    @pl.when(j == 0)
    def _():
        assemble(r, (own, a, b, c, d), cat)

    gs[...] = dot(cat[...], wg[...])
    us[...] = dot(cat[...], wu[...])
    step = 256
    for at in range(0, gs.shape[0], step):
        gate, up = gs[at : at + step, :], us[at : at + step, :]
        sig = jax.nn.sigmoid(gate)
        silu = gate * sig
        hid[at : at + step, :] = (silu * up).astype(BF16)
        act[at : at + step, :] = silu.astype(act.dtype)
        slope[at : at + step, :] = (up * sig * (1.0 + gate * (1.0 - sig))).astype(slope.dtype)
    part = dot(hid[...], wd[...])

    @pl.when(j == 0)
    def _():
        total[...] = part

    @pl.when(j > 0)
    def _():
        total[...] += part

    @pl.when(j == pl.num_programs(0) - 1)
    def _():
        split_out(r, total, own.shape[1], (sa, ka, sb, kb))


def backward_kernel(ids, own, a, b, c, d, wg, wu, wd, act, slope, cat, dgate, dup, sa, ka, sb, kb, total, dh):
    j = pl.program_id(0)
    r = ids[2]

    @pl.when(j == 0)
    def _():
        assemble(r, (own, a, b, c, d), cat)

    dh[...] = dot(cat[...], wd[...], ((1,), (1,)))
    step = 256
    for at in range(0, dh.shape[0], step):
        piece = dh[at : at + step, :]
        dgate[at : at + step, :] = (piece * slope[at : at + step, :].astype(F32)).astype(BF16)
        dup[at : at + step, :] = (piece * act[at : at + step, :].astype(F32)).astype(BF16)
    part = dot(dgate[...], wg[...], ((1,), (1,))) + dot(dup[...], wu[...], ((1,), (1,)))

    @pl.when(j == 0)
    def _():
        total[...] = part

    @pl.when(j > 0)
    def _():
        total[...] += part

    @pl.when(j == pl.num_programs(0) - 1)
    def _():
        split_out(r, total, own.shape[1], (sa, ka, sb, kb))


def weights_kernel(xcat, gcat, dgate, dup, hid, ggate, gup, gdown, turned):
    @pl.when(pl.program_id(0) == 0)
    def _():
        turned[...] = jnp.transpose(xcat[...])

    ggate[...] = dot(turned[...], dgate[...])
    gup[...] = dot(turned[...], dup[...])
    gdown[...] = dot(hid[...], gcat[...], ((0,), (0,)))


def middle_kernel(ka, ra, kb, rb, sa, sb, kept):
    half, feats = sa.shape
    kept[0:half, :] = ka[:, 0:feats].astype(F32) + ra[:, 0:feats].astype(F32)
    kept[half : 2 * half, :] = kb[:, 0:feats].astype(F32) + rb[:, 0:feats].astype(F32)
    sa[...] = (ka[:, feats:].astype(F32) + ra[:, feats:].astype(F32)).astype(BF16)
    sb[...] = (kb[:, feats:].astype(F32) + rb[:, feats:].astype(F32)).astype(BF16)


def last_kernel(kept, ra, rb, y0, y1, y2, y3):
    half = ra.shape[0]
    size = y0.shape[0]
    for q, out in enumerate((y0, y1, y2, y3)):
        at = q * size
        other = ra[at : at + size, :] if at < half else rb[at - half : at - half + size, :]
        out[...] = (kept[at : at + size, :] + other.astype(F32)).astype(BF16)


def shift(x, axis, bit):
    n = lax.axis_size(axis)
    return lax.ppermute(x, axis, [(i, i ^ bit) for i in range(n)])


def sds(shape, dtype):
    return jax.ShapeDtypeStruct(shape, dtype)


def gather_quad(x):
    half = x.shape[0] // 2
    a = shift(x, "rep", 1)
    b = shift(x, "rep", 2)
    c = shift(a[:half], "rep", 2)
    d = shift(b[half:], "rep", 1)
    return x, a, b, c, d


def reduce_quad(sa, ka, sb, kb):
    ra = shift(sa, "rep", 1)
    rb = shift(sb, "rep", 2)
    half, feats = sa.shape[0], sa.shape[1] // 2
    piece = sds((half, feats), BF16)
    ma, mb, kept = pl.pallas_call(
        middle_kernel,
        out_shape=(piece, piece, sds((2 * half, feats), F32)),
        compiler_params=params(),
        name="reduce_middle",
    )(ka, ra, kb, rb)
    fa = shift(ma, "rep", 2)
    fb = shift(mb, "rep", 1)
    quarter = sds((half // 2, feats), BF16)
    return pl.pallas_call(
        last_kernel,
        out_shape=(quarter,) * 4,
        compiler_params=params(),
        name="reduce_last",
    )(kept, fa, fb)


def over_chips(chunks):
    return [chunks[q] if q == 0 else shift(chunks[q], "exp", 2 * q) for q in range(CHIPS)]


def on_quad(tokens, routes, probs, capacity, plan, grad_out, w_gate, w_up, w_down):
    toks, feats = tokens.shape
    per = 4 * toks // capacity.shape[0]
    wg, wu, wd = w_gate[0], w_up[0], w_down[0]
    width, ff = wg.shape
    rows = 2 * per * CHIPS
    me = lax.axis_index("exp").astype(I32)
    ids = jnp.stack([me // 2, me % 2, lax.axis_index("rep").astype(I32)])
    own_m = jnp.concatenate(
        [routes.T.astype(F32), probs.T, jnp.zeros((4, toks), F32)], axis=0
    )
    par_m = shift(own_m, "exp", 1)
    par_x = shift(tokens, "exp", 1)
    par_g = shift(grad_out, "exp", 1)

    near = sds((2 * per, feats), BF16)
    far = sds((2 * per + 16, feats), BF16)
    xc = pl.pallas_call(
        functools.partial(x_kernel, per),
        in_specs=[smem()] + [vmem()] * 4,
        out_shape=(near, far, far, far),
        compiler_params=params(),
        name="send_tokens",
    )(ids, own_m, par_m, tokens, par_x)
    xr = over_chips(xc)
    whole = pl.BlockSpec((8, toks), lambda i: (0, 0))
    block = pl.BlockSpec((toks, feats), lambda i: (0, 0))
    tail = pl.BlockSpec((16, feats), lambda i: (2 * per // 16, 0))
    gc = pl.pallas_call(
        functools.partial(g_kernel, per, 2 * toks),
        grid=(1,),
        in_specs=[smem()] * 3 + [whole] * 2 + [tail] * 3 + [block] * 2,
        out_specs=[pl.BlockSpec((2 * per, feats), lambda i: (0, 0))] * 4
        + [pl.BlockSpec((toks, 128), lambda i: (0, 0))],
        out_shape=(near,) * 4 + (sds((toks, 128), F32),),
        compiler_params=params(),
        name="send_grads",
    )(ids, capacity, plan, own_m, par_m, xr[1], xr[2], xr[3], grad_out, par_g)
    info = gc[4]
    gr = over_chips(gc[:4])

    xs = gather_quad(jnp.concatenate([xr[0]] + [x[: 2 * per] for x in xr[1:]], axis=0))
    gs = gather_quad(jnp.concatenate(gr, axis=0))

    jb = 256
    steps = ff // jb
    shards = [
        pl.BlockSpec((rows, feats), lambda j: (0, 0)),
        pl.BlockSpec((rows, feats), lambda j: (0, 0)),
        pl.BlockSpec((rows, feats), lambda j: (0, 0)),
        pl.BlockSpec((rows // 2, feats), lambda j: (0, 0)),
        pl.BlockSpec((rows // 2, feats), lambda j: (0, 0)),
    ]
    w_col = pl.BlockSpec((width, jb), lambda j: (0, j))
    w_row = pl.BlockSpec((jb, width), lambda j: (j, 0))
    full = pl.BlockSpec((rows, width), lambda j: (0, 0))
    col = pl.BlockSpec((rows, jb), lambda j: (0, j))
    pair = pl.BlockSpec((rows // 2, 2 * feats), lambda j: (0, 0))
    pair_t = sds((rows // 2, 2 * feats), BF16)
    inner = sds((rows, ff), BF16)
    xcat, hid, act, slope, *out_parts = pl.pallas_call(
        forward_kernel,
        grid=(steps,),
        in_specs=[smem()] + shards + [w_col, w_col, w_row],
        out_specs=[full, col, col, col] + [pair] * 4,
        out_shape=(sds((rows, width), BF16), inner, inner, inner) + (pair_t,) * 4,
        scratch_shapes=[
            pltpu.VMEM((rows, width), F32),
            pltpu.VMEM((rows, jb), F32),
            pltpu.VMEM((rows, jb), F32),
        ],
        compiler_params=params(),
        cost_estimate=pl.CostEstimate(
            flops=6 * rows * width * ff, bytes_accessed=24 * rows * width, transcendentals=rows * ff
        ),
        name="forward",
    )(ids, *xs, wg, wu, wd)
    y = reduce_quad(*out_parts)

    gcat, dgate, dup, *dx_parts = pl.pallas_call(
        backward_kernel,
        grid=(steps,),
        in_specs=[smem()] + shards + [w_col, w_col, w_row, col, col],
        out_specs=[full, col, col] + [pair] * 4,
        out_shape=(sds((rows, width), BF16), inner, inner) + (pair_t,) * 4,
        scratch_shapes=[pltpu.VMEM((rows, width), F32), pltpu.VMEM((rows, jb), F32)],
        compiler_params=params(),
        cost_estimate=pl.CostEstimate(
            flops=6 * rows * width * ff, bytes_accessed=24 * rows * width, transcendentals=0
        ),
        name="backward",
    )(ids, *gs, wg, wu, wd, act, slope)
    dx = reduce_quad(*dx_parts)

    grad_gate, grad_up, grad_down = pl.pallas_call(
        weights_kernel,
        grid=(steps,),
        in_specs=[full, full, col, col, col],
        out_specs=[w_col, w_col, w_row],
        out_shape=(sds((width, ff), F32), sds((width, ff), F32), sds((ff, width), F32)),
        scratch_shapes=[pltpu.VMEM((width, rows), BF16)],
        compiler_params=params(),
        cost_estimate=pl.CostEstimate(
            flops=6 * rows * width * ff, bytes_accessed=24 * rows * width, transcendentals=0
        ),
        name="weight_grads",
    )(xcat, gcat, dgate, dup, hid)

    yr = over_chips(y)
    wide = sds((toks, feats + 128), F32)
    kept, sent = pl.pallas_call(
        functools.partial(back_kernel, per, True),
        out_shape=(wide, wide),
        compiler_params=params(),
        name="combine_out",
    )(*yr, info, grad_out, par_g)
    got = shift(sent, "exp", 1)
    both = kept + got
    mixed = both[:, :feats].astype(BF16)
    dots = both[:, feats : feats + 2].T
    dots = dots + shift(dots, "rep", 1)
    dots = dots + shift(dots, "rep", 2)
    grad_probs = dots.T

    dr = over_chips(dx)
    flat = sds((toks, feats), F32)
    kept, sent = pl.pallas_call(
        functools.partial(back_kernel, per, False),
        out_shape=(flat, flat),
        compiler_params=params(),
        name="combine_grad",
    )(*dr, info)
    grad_tokens = (kept + shift(sent, "exp", 1)).astype(BF16)
    return (mixed, grad_tokens, grad_probs, grad_gate[None], grad_up[None], grad_down[None])


def solution(mesh):
    sizes = dict(mesh.shape)
    fast = sizes["rep"] == 4 and sizes["exp"] == 8
    return jax.shard_map(
        on_quad if fast else on_device,
        mesh=mesh,
        in_specs=(
            P("exp", "rep"),
            P("exp", None),
            P("exp", None),
            P(),
            P(),
            P("exp", "rep"),
            P("exp", None, "rep"),
            P("exp", None, "rep"),
            P("exp", "rep", None),
        ),
        out_specs=(
            P("exp", "rep"),
            P("exp", "rep"),
            P("exp", None),
            P("exp", None, "rep"),
            P("exp", None, "rep"),
            P("exp", "rep", None),
        ),
        check_vma=False,
    )
```

```python
import functools

import jax
import jax.numpy as jnp
from jax import lax
from jax.experimental import pallas as pl
from jax.experimental.pallas import tpu as pltpu
from jax.sharding import PartitionSpec as P

HOT = 4


def carried_in(value, axis, combine, identity):
    peers, mine = (lax.axis_size(axis), lax.axis_index(axis))
    everything = lax.all_gather(value, axis)
    start = jnp.broadcast_to(jnp.asarray(identity, value.dtype), value.shape)

    def step(k, before):
        reached = k < mine
        new = combine(before, everything[k])
        return jnp.where(reached, new, before)

    return lax.fori_loop(0, peers, step, start)


def fill_rows(shard, flat, rank, token_of, scale, experts, per_slot):
    picked = shard[token_of]
    if scale is not None:
        picked = (picked.astype(jnp.float32) * scale[:, None]).astype(jnp.bfloat16)
    empty = jnp.zeros((experts, per_slot, shard.shape[1]), jnp.bfloat16)
    return empty.at[flat, rank].set(picked)


def dispatch(shard, flat, rank, token_of, scale, experts, per_slot):
    buffer = fill_rows(shard, flat, rank, token_of, scale, experts, per_slot)
    received = lax.all_to_all(buffer, "exp", split_axis=0, concat_axis=0, tiled=True)
    narrow = received.reshape(-1, received.shape[2])
    return lax.all_gather(narrow, "rep", axis=1, tiled=True)


def return_rows(rows, flat, rank, experts, per_slot):
    back = lax.all_to_all(
        rows.reshape(experts, per_slot, rows.shape[1]),
        "exp",
        split_axis=0,
        concat_axis=0,
        tiled=True,
    )
    return back[flat, rank].astype(jnp.float32)


def on_device(tokens, routes, probs, capacity, plan, grad_out, w_gate, w_up, w_down):
    tok_rows = tokens.shape[0]
    experts = capacity.shape[0]
    per_slot = 4 * tok_rows // experts
    feat_cols = tokens.shape[1]
    flat = routes.reshape(-1)
    expert_ids = jnp.arange(experts, dtype=jnp.int32)
    onehot = (flat[:, None] == expert_ids[None, :]).astype(jnp.int32)
    rank = jnp.sum((jnp.cumsum(onehot, axis=0) - onehot) * onehot, axis=1)
    counts = jnp.sum(onehot, axis=0)
    earlier = carried_in(
        counts, "exp", lambda first, second: first + second, jnp.zeros_like(counts)
    )
    position = rank + jnp.sum(onehot * earlier[None, :], axis=1)
    hot_flag = jnp.any(plan[:HOT][:, None] == expert_ids[None, :], axis=0).astype(jnp.int32)
    limit = capacity + 2 * tok_rows * hot_flag
    keep = (position < jnp.sum(onehot * limit[None, :], axis=1)).astype(jnp.float32)
    weight = probs.reshape(-1) * keep
    token_of = jnp.arange(2 * tok_rows, dtype=jnp.int32) // 2
    wg = w_gate[0]
    wu = w_up[0]
    wd = w_down[0]
    xs = dispatch(tokens, flat, rank, token_of, None, experts, per_slot)
    gate = jnp.dot(xs, wg, preferred_element_type=jnp.float32)
    up = jnp.dot(xs, wu, preferred_element_type=jnp.float32)
    sig = jax.nn.sigmoid(gate)
    silu = gate * sig
    hidden = (silu * up).astype(jnp.bfloat16)
    partial_value = jnp.dot(hidden, wd, preferred_element_type=jnp.float32)
    out_rows = lax.psum_scatter(
        partial_value.astype(jnp.bfloat16), "rep", scatter_dimension=1, tiled=True
    )
    picked = return_rows(out_rows, flat, rank, experts, per_slot)
    mixed = jnp.sum((weight[:, None] * picked).reshape(tok_rows, 2, feat_cols), axis=1).astype(
        jnp.bfloat16
    )
    dots = jnp.sum(grad_out[token_of].astype(jnp.float32) * picked, axis=1)
    dots = lax.psum(dots, "rep")
    grad_probs = (keep * dots).reshape(tok_rows, 2)
    dout = dispatch(grad_out, flat, rank, token_of, weight, experts, per_slot)
    dh = lax.dot_general(dout, wd, (((1,), (1,)), ((), ())), preferred_element_type=jnp.float32)
    dgate = (dh * up * sig * (1.0 + gate * (1.0 - sig))).astype(jnp.bfloat16)
    dup = (dh * silu).astype(jnp.bfloat16)
    grad_down = lax.dot_general(
        hidden, dout, (((0,), (0,)), ((), ())), preferred_element_type=jnp.float32
    )
    grad_gate = lax.dot_general(
        xs, dgate, (((0,), (0,)), ((), ())), preferred_element_type=jnp.float32
    )
    grad_up = lax.dot_general(xs, dup, (((0,), (0,)), ((), ())), preferred_element_type=jnp.float32)
    dpartial = lax.dot_general(
        dgate, wg, (((1,), (1,)), ((), ())), preferred_element_type=jnp.float32
    )
    dpartial = dpartial + lax.dot_general(
        dup, wu, (((1,), (1,)), ((), ())), preferred_element_type=jnp.float32
    )
    dx_rows = lax.psum_scatter(
        dpartial.astype(jnp.bfloat16), "rep", scatter_dimension=1, tiled=True
    )
    back = return_rows(dx_rows, flat, rank, experts, per_slot)
    grad_tokens = jnp.sum((weight[:, None] * back).reshape(tok_rows, 2, feat_cols), axis=1).astype(
        jnp.bfloat16
    )
    return (mixed, grad_tokens, grad_probs, grad_gate[None], grad_up[None], grad_down[None])


F32 = jnp.float32
BF16 = jnp.bfloat16
I32 = jnp.int32
CHIPS = 4
VMEM_BYTES = 24 * 1024 * 1024


def dot(a, b, dims=((1,), (0,))):
    return lax.dot_general(a, b, (dims, ((), ())), preferred_element_type=F32)


def params(**kw):
    return pltpu.CompilerParams(vmem_limit_bytes=VMEM_BYTES, **kw)


def vmem():
    return pl.BlockSpec(memory_space=pltpu.VMEM)


def smem():
    return pl.BlockSpec(memory_space=pltpu.SMEM)


def place_rows(ids, own, par, per):
    z, c = ids[0], ids[1]
    toks = own.shape[1]
    row = lax.broadcasted_iota(I32, (2 * CHIPS, toks), 0)
    expert = 2 * (z ^ (row % CHIPS)) + c
    first = row < CHIPS
    named = [
        jnp.where(first, own[k : k + 1, :], par[k : k + 1, :]).astype(I32) == expert
        for k in range(2)
    ]
    either = jnp.logical_or(named[0], named[1])
    before = lax.broadcasted_iota(I32, (toks, toks), 0) < lax.broadcasted_iota(
        I32, (toks, toks), 1
    )
    rank = dot(either.astype(F32).astype(BF16), before.astype(F32).astype(BF16)).astype(I32)
    return row, expert, named, either, rank


def pick(rank, either, i, per):
    at = jnp.where(either[i : i + 1, :], rank[i : i + 1, :], -1)
    slots = lax.broadcasted_iota(I32, (per, at.shape[1]), 0)
    return (slots == at).astype(F32)


def thirds(line):
    high = line.astype(BF16).astype(F32)
    middle = (line - high).astype(BF16).astype(F32)
    return high, middle, line - high - middle


def send_kernel(per, ids, own_x, own_g, own_m, par_m, par_x, par_g, x0, x1, x2, x3, g0, g1, g2, g3):
    own, par = own_m[...], par_m[...]
    toks = own.shape[1]
    _, _, _, either, rank = place_rows(ids, own, par, per)
    tail = lax.broadcasted_iota(I32, (16, toks), 0)
    lines = [own[0:1, :], own[1:2, :], par[0:1, :], par[1:2, :]]
    for table in (own, par):
        for k in range(2):
            lines += thirds(table[2 + k : 3 + k, :])
    extra = jnp.zeros((16, toks), F32)
    for i, line in enumerate(lines):
        extra = jnp.where(tail == i, line, extra)
    for q in range(CHIPS):
        for src in range(2):
            hot = pick(rank, either, CHIPS * src + q, per).astype(BF16)
            place = slice(src * per, (src + 1) * per)
            (x0, x1, x2, x3)[q][place, :] = dot(hot, (own_x, par_x)[src][...]).astype(BF16)
            (g0, g1, g2, g3)[q][place, :] = dot(hot, (own_g, par_g)[src][...]).astype(BF16)
        if q:
            (x0, x1, x2, x3)[q][2 * per : 2 * per + 16, :] = extra.astype(BF16)


def room_of(e, cap, plan, extra_slots):
    room = cap[e]
    for h in range(HOT):
        room = room + jnp.where(plan[h] == e, extra_slots, 0)
    return room


def place_kernel(per, extra_slots, ids, cap, plan, own_m, par_m, e1, e2, e3, info, scale):
    own, par = own_m[...], par_m[...]
    toks = own.shape[1]
    z, c = ids[0], ids[1]
    row, expert, named, either, rank = place_rows(ids, own, par, per)
    q_col = row[:, 0:1] % CHIPS
    first = row < CHIPS
    first_col = first[:, 0:1]

    sources = []
    for s, table in enumerate((own, par)):
        sources.append((0, s, [table[k : k + 1, :] for k in range(4)]))
    for p, ref in ((1, e1), (2, e2), (3, e3)):
        table = ref[2 * per : 2 * per + 16, :].astype(F32)
        for s in range(2):
            lines = [table[2 * s + k : 2 * s + k + 1, :] for k in range(2)]
            for k in range(2):
                at = 4 + 3 * (2 * s + k)
                lines.append(
                    table[at : at + 1, :] + table[at + 1 : at + 2, :] + table[at + 2 : at + 3, :]
                )
            sources.append((p, s, lines))

    limit = jnp.zeros((2 * CHIPS, 1), I32)
    for q in range(CHIPS):
        limit = jnp.where(q_col == q, room_of(2 * (z ^ q) + c, cap, plan, extra_slots), limit)
    earlier = jnp.zeros((2 * CHIPS, 1), F32)
    for p, s, lines in sources:
        hits = jnp.logical_or(lines[0].astype(I32) == expert, lines[1].astype(I32) == expert)
        count = jnp.sum(hits.astype(F32), axis=1, keepdims=True)
        block = 2 * (z ^ p) + (c ^ s)
        ahead = jnp.where(
            first_col,
            (block < 2 * z + c).astype(F32),
            (block < 2 * z + (c ^ 1)).astype(F32),
        )
        earlier = earlier + count * ahead
    keep = jnp.where(rank + earlier.astype(I32) < limit, 1.0, 0.0)
    kinds = []
    for k in range(2):
        prob = jnp.where(first, own[2 + k : 3 + k, :], par[2 + k : 3 + k, :])
        mine = named[k].astype(F32)
        slot = (row % CHIPS * per + rank + 1).astype(F32)
        kinds.append((mine * slot, mine * keep * prob, mine * keep))
    at = lax.broadcasted_iota(I32, (128, toks), 0)
    table = jnp.zeros((128, toks), F32)
    for kind in range(3):
        for src in range(2):
            half = first if src == 0 else jnp.logical_not(first)
            for k in range(2):
                line = jnp.sum(jnp.where(half, kinds[k][kind], 0.0), axis=0, keepdims=True)
                table = jnp.where(at == 4 * kind + 2 * src + k, line, table)
    info[...] = jnp.transpose(table)

    stacked = [jnp.zeros((2 * CHIPS, toks), F32) for _ in range(4)]
    blocks = jnp.zeros((2 * CHIPS, 1), I32)
    for p, s, lines in sources:
        i = 2 * p + s
        stacked = [jnp.where(row == i, line, old) for line, old in zip(lines, stacked)]
        blocks = jnp.where(row[:, 0:1] == i, 2 * (z ^ p) + (c ^ s), blocks)
    mine = 2 * z + c
    named = [stacked[k].astype(I32) == mine for k in range(2)]
    either = jnp.logical_or(named[0], named[1])
    before = lax.broadcasted_iota(I32, (toks, toks), 0) < lax.broadcasted_iota(
        I32, (toks, toks), 1
    )
    hits = either.astype(F32)
    rank = dot(hits.astype(BF16), before.astype(F32).astype(BF16)).astype(I32)
    count = jnp.sum(hits, axis=1, keepdims=True)
    earlier = jnp.zeros((2 * CHIPS, 1), F32)
    for p, s, _ in sources:
        i = 2 * p + s
        ahead = (2 * (z ^ p) + (c ^ s) < blocks).astype(F32)
        earlier = earlier + ahead * count[i : i + 1, :]
    keep = rank + earlier.astype(I32) < room_of(mine, cap, plan, extra_slots)
    weight = jnp.where(keep, 1.0, 0.0) * (
        named[0].astype(F32) * stacked[2] + named[1].astype(F32) * stacked[3]
    )
    for i in range(2 * CHIPS):
        hot = pick(rank, either, i, per)
        value = jnp.sum(hot * weight[i : i + 1, :], axis=1, keepdims=True)
        scale[i * per : (i + 1) * per, :] = jnp.broadcast_to(value, (per, 128))


def load_kernel(a, b, c, x, y, z, sems):
    copies = [
        pltpu.make_async_copy(src, dst, sems.at[i])
        for i, (src, dst) in enumerate(((a, x), (b, y), (c, z)))
    ]
    for copy in copies:
        copy.start()
    for copy in copies:
        copy.wait()


def combine(per, src, k, rows, info):
    slot = info[:, 2 * src + k : 2 * src + k + 1].astype(I32) - 1
    slots = lax.broadcasted_iota(I32, (info.shape[0], CHIPS * per), 1)
    return dot((slots == slot).astype(F32).astype(BF16), rows)


def back_kernel(per, with_dots, y0, y1, y2, y3, info_ref, *refs):
    if with_dots:
        own_g, par_g, kept, sent = refs
    else:
        kept, sent = refs
    info = info_ref[...]
    feats = y0.shape[1]
    toks = info.shape[0]
    lane = lax.broadcasted_iota(I32, (toks, 128), 1)
    for src, out in enumerate((kept, sent)):
        rows = jnp.concatenate([y[src * per : (src + 1) * per, :] for y in (y0, y1, y2, y3)], axis=0)
        total = jnp.zeros((toks, feats), F32)
        dots = jnp.zeros((toks, 128), F32)
        for k in range(2):
            picked = combine(per, src, k, rows, info)
            at = 2 * src + k
            total = total + info[:, 4 + at : 5 + at] * picked
            if with_dots:
                grad = (own_g, par_g)[src][...].astype(F32)
                inner = jnp.sum(grad * picked, axis=1, keepdims=True) * info[:, 8 + at : 9 + at]
                dots = jnp.where(lane == k, inner, dots)
        out[:, 0:feats] = total
        if with_dots:
            out[:, feats : feats + 128] = dots


def assemble(r, at, shards, cat):
    own, a, b, c, d = shards
    rows, feats = own.shape
    half = rows // 2

    def cols(k):
        return pl.ds(pl.multiple_of((r ^ k) * feats, feats), feats)

    cat[at : at + rows, cols(0)] = own[...]
    cat[at : at + rows, cols(1)] = a[...]
    cat[at : at + rows, cols(2)] = b[...]
    cat[at : at + half, cols(3)] = c[...]
    cat[at + half : at + rows, cols(3)] = d[...]


def split_out(part, groups):
    _, (send, *_) = groups[0]
    feats = send.shape[1] // 2
    low, high = slice(0, feats), slice(feats, 2 * feats)
    for k in (3, 1, 2, 0):
        piece = part(k).astype(BF16)
        for at, (send_a, keep_a, send_b, keep_b) in groups:
            half = send_a.shape[0]
            top = ((keep_a, low), (send_a, low), (keep_a, high), (send_a, high))[k]
            bottom = ((keep_b, low), (keep_b, high), (send_b, low), (send_b, high))[k]
            top[0][:, top[1]] = piece[at : at + half, :]
            bottom[0][:, bottom[1]] = piece[at + half : at + 2 * half, :]


def forward_kernel(ids, *refs):
    near, far, (wg, wu, cat, hid, act, slope) = refs[:5], refs[5:10], refs[10:]
    r = ids[2]
    assemble(r, 0, near, cat)
    assemble(r, near[0].shape[0], far, cat)
    step = 256
    for j in range(0, hid.shape[1], step):
        cols = slice(j, j + step)
        gate = dot(cat[...], wg[:, cols])
        up = dot(cat[...], wu[:, cols])
        sig = jax.nn.sigmoid(gate)
        silu = gate * sig
        hid[:, cols] = (silu * up).astype(BF16)
        act[:, cols] = silu.astype(BF16)
        slope[:, cols] = (up * (sig + silu * (1.0 - sig))).astype(BF16)


def out_kernel(ids, hid, wd, sa, ka, sb, kb):
    r = ids[2]
    feats = sa.shape[1] // 2

    def part(k):
        return dot(hid[...], wd[:, pl.ds(pl.multiple_of((r ^ k) * feats, feats), feats)])

    split_out(part, [(0, (sa, ka, sb, kb))])


def backward_kernel(ids, own, a, b, c, d, wg, wu, wd, act, slope, cat, dgate, dup, *outs):
    r = ids[2]
    assemble(r, 0, (own, a, b, c, d), cat)
    step = 256
    for j in range(0, dgate.shape[1], step):
        cols = slice(j, j + step)
        dh = dot(cat[...], wd[cols, :], ((1,), (1,)))
        dgate[:, cols] = (dh * slope[:, cols].astype(F32)).astype(BF16)
        dup[:, cols] = (dh * act[:, cols].astype(F32)).astype(BF16)

    def part(k):
        feats = own.shape[1]
        line = pl.ds(pl.multiple_of((r ^ k) * feats, feats), feats)
        return dot(dgate[...], wg[line, :], ((1,), (1,))) + dot(dup[...], wu[line, :], ((1,), (1,)))

    split_out(part, [(cat.shape[0] // 2, outs[:4]), (0, outs[4:])])


def weights_kernel(xcat, gcat, dgate, dup, hid, ggate, gup, gdown, done):
    done[...] = jnp.zeros_like(done)
    size = ggate.shape[0]
    cols = pl.ds(pl.multiple_of(pl.program_id(0) * size, size), size)
    x = xcat[:, cols]
    ggate[...] = dot(x, dgate[...], ((0,), (0,)))
    gup[...] = dot(x, dup[...], ((0,), (0,)))
    gdown[...] = dot(hid[:, cols], gcat[...], ((0,), (0,)))


def join_kernel(a, b, out):
    size = out.shape[0] // 2
    out[0:size, :] = a[0:size, :]
    out[size : 2 * size, :] = b[0:size, :]


def join_scaled_kernel(a, b, c, d, scale, out):
    size = out.shape[0] // CHIPS
    for q, ref in enumerate((a, b, c, d)):
        at = slice(q * size, (q + 1) * size)
        out[at, :] = (ref[...].astype(F32) * scale[at, 0:1]).astype(BF16)


def middle_kernel(ka, ra, kb, rb, sa, sb, kept):
    half, feats = sa.shape
    kept[0:half, :] = ka[:, 0:feats].astype(F32) + ra[:, 0:feats].astype(F32)
    kept[half : 2 * half, :] = kb[:, 0:feats].astype(F32) + rb[:, 0:feats].astype(F32)
    sa[...] = (ka[:, feats:].astype(F32) + ra[:, feats:].astype(F32)).astype(BF16)
    sb[...] = (kb[:, feats:].astype(F32) + rb[:, feats:].astype(F32)).astype(BF16)


def last_kernel(kept, ra, rb, *outs):
    half = ra.shape[0]
    size = outs[0].shape[0]
    for q, out in enumerate(outs):
        at = q * size
        other = ra[at : at + size, :] if at < half else rb[at - half : at - half + size, :]
        out[...] = (kept[at : at + size, :] + other.astype(F32)).astype(BF16)


def shift(x, axis, bit):
    n = lax.axis_size(axis)
    return lax.ppermute(x, axis, [(i, i ^ bit) for i in range(n)])


def sds(shape, dtype):
    return jax.ShapeDtypeStruct(shape, dtype)


def vm(shape, dtype):
    return pltpu.VMEM(shape, dtype)


def pin(*arrays):
    return [pltpu.with_memory_space_constraint(x, pltpu.VMEM) for x in arrays]


def kernel_call(body, name, outs, *args, plan_args=0, loose=0, flops=0, after=()):
    count = len(args)
    pinned = list(args[: plan_args + loose]) + pin(*args[plan_args + loose :], *after)

    def run(*refs):
        body(*refs[:count], *refs[count + len(after) :])

    return pl.pallas_call(
        run,
        in_specs=[smem()] * plan_args + [vmem()] * (count - plan_args + len(after)),
        out_shape=outs,
        compiler_params=params(),
        cost_estimate=pl.CostEstimate(flops=flops, bytes_accessed=1 << 20, transcendentals=0),
        name=name,
    )(*pinned)


def relay_kernel(a, b, top, bottom):
    half = top.shape[0]
    top[...] = a[0:half, :]
    bottom[...] = b[half : 2 * half, :]


def gather_first(x):
    return x, shift(x, "rep", 1), shift(x, "rep", 2)


def gather_second(parts, after):
    x, a, b = parts
    half = vm((x.shape[0] // 2, x.shape[1]), BF16)
    top, bottom = kernel_call(relay_kernel, "relay", (half, half), a, b, after=after)
    return x, a, b, shift(top, "rep", 2), shift(bottom, "rep", 1)


def reduce_first(sa, ka, sb, kb):
    return ka, shift(sa, "rep", 1), kb, shift(sb, "rep", 2)


def reduce_second(parts, after=()):
    half, feats = parts[0].shape[0], parts[0].shape[1] // 2
    piece = vm((half, feats), BF16)
    ma, mb, kept = kernel_call(
        middle_kernel, "reduce_middle", (piece, piece, vm((2 * half, feats), F32)), *parts, after=after
    )
    return kept, shift(ma, "rep", 2), shift(mb, "rep", 1)


def reduce_last(parts, size, after=()):
    rows, feats = parts[0].shape
    outs = (vm((size, feats), BF16),) * (rows // size)
    return kernel_call(last_kernel, "reduce_last", outs, *parts, after=after)


def over_chips(chunks):
    return [chunks[q] if q == 0 else shift(chunks[q], "exp", 2 * q) for q in range(CHIPS)]


def on_quad(tokens, routes, probs, capacity, plan, grad_out, w_gate, w_up, w_down):
    toks, feats = tokens.shape
    per = 4 * toks // capacity.shape[0]
    wg, wu, wd = w_gate[0], w_up[0], w_down[0]
    width, ff = wg.shape
    rows = 2 * per * CHIPS
    me = lax.axis_index("exp").astype(I32)
    ids = jnp.stack([me // 2, me % 2, lax.axis_index("rep").astype(I32)])
    own_m = jnp.concatenate(
        [routes.T.astype(F32), probs.T, jnp.zeros((4, toks), F32)], axis=0
    )
    par_m = shift(own_m, "exp", 1)
    par_x = shift(tokens, "exp", 1)
    par_g = shift(grad_out, "exp", 1)

    size = 2 * per
    near = vm((size, feats), BF16)
    far = vm((size + 16, feats), BF16)
    sent = kernel_call(
        functools.partial(send_kernel, per),
        "send",
        (near, far, far, far) + (near,) * 4,
        ids, tokens, grad_out, own_m, par_m, par_x, par_g,
        plan_args=1,
        loose=2,
    )
    xr = over_chips(sent[:CHIPS])
    gr = over_chips(sent[CHIPS:])
    loaded = vm((width, ff), BF16)
    wg, wu, wd = pl.pallas_call(
        load_kernel,
        in_specs=[pl.BlockSpec(memory_space=pltpu.HBM)] * 3,
        out_shape=(loaded, loaded, vm((ff, width), BF16)),
        scratch_shapes=[pltpu.SemaphoreType.DMA((3,))],
        compiler_params=params(),
        name="load_weights",
    )(*[pltpu.with_memory_space_constraint(w, pltpu.HBM) for w in (wg, wu, wd)])
    pair_rows = vm((2 * size, feats), BF16)
    xa = gather_first(kernel_call(join_kernel, "join_near", pair_rows, xr[0], xr[1]))
    xb = gather_first(kernel_call(join_kernel, "join_far", pair_rows, xr[2], xr[3], after=(wg,)))
    info, scale = kernel_call(
        functools.partial(place_kernel, per, 2 * toks),
        "place",
        (vm((toks, 128), F32), vm((rows, 128), F32)),
        ids, capacity, plan, own_m, par_m, *xr[1:],
        plan_args=3,
    )
    xa = gather_second(xa, (info, xb[0]))
    xb = gather_second(xb, gr[1:])
    gs = gather_first(
        kernel_call(join_scaled_kernel, "join_grads", vm((rows, feats), BF16), *gr, scale)
    )

    pair_t = vm((rows // 2, 2 * feats), BF16)
    inner = vm((rows, ff), BF16)
    wide = vm((rows, width), BF16)
    work = 2 * rows * width * ff
    xcat, hid, act, slope = kernel_call(
        forward_kernel,
        "forward",
        (wide, inner, inner, inner),
        ids, *xa, *xb, wg, wu,
        plan_args=1,
        flops=2 * work,
        after=gs[:1],
    )
    gs = gather_second(gs, (hid,))
    out_parts = kernel_call(
        out_kernel, "out_parts", (pair_t,) * 4, ids, hid, wd, plan_args=1, flops=work, after=gs[3:]
    )
    out_sums = reduce_second(reduce_first(*out_parts))

    gcat, dgate, dup, *dx_parts = kernel_call(
        backward_kernel,
        "backward",
        (wide, inner, inner) + (vm((size, 2 * feats), BF16),) * 8,
        ids, *gs, wg, wu, wd, act, slope,
        plan_args=1,
        flops=3 * work,
        after=out_parts[:1],
    )
    far_first = reduce_first(*dx_parts[:4])
    near_first = reduce_first(*dx_parts[4:])

    steps = 4
    grad_gate, grad_up, grad_down, done = pl.pallas_call(
        weights_kernel,
        grid=(steps,),
        in_specs=[vmem()] * 5,
        out_specs=[pl.BlockSpec((n // steps, m), lambda i: (i, 0)) for n, m in ((width, ff), (width, ff), (ff, width))] + [vmem()],
        out_shape=(sds((width, ff), F32), sds((width, ff), F32), sds((ff, width), F32), vm((8, 128), F32)),
        compiler_params=params(),
        cost_estimate=pl.CostEstimate(flops=3 * work, bytes_accessed=12 << 20, transcendentals=0),
        name="weight_grads",
    )(*pin(xcat, gcat, dgate, dup, hid))

    far_sums = reduce_second(far_first, (done, out_sums[0]))
    near_sums = reduce_second(near_first, (far_sums[0],))
    yr = over_chips(reduce_last(out_sums, size, (near_sums[0],)))
    dx_far = reduce_last(far_sums, size, yr[:1])
    dx_near = reduce_last(near_sums, size, dx_far[:1])
    dr = over_chips([*dx_near, *dx_far])
    broad = vm((toks, feats + 128), F32)
    kept, sent = kernel_call(
        functools.partial(back_kernel, per, True),
        "combine_out",
        (broad, broad),
        *yr, info, grad_out, par_g,
        after=dx_near[:1],
    )
    both = kept + shift(sent, "exp", 1)
    mixed = both[:, :feats].astype(BF16)
    dots = both[:, feats : feats + 2].T
    dots = dots + shift(dots, "rep", 1)
    dots = dots + shift(dots, "rep", 2)
    grad_probs = dots.T

    flat = vm((toks, feats), F32)
    kept, sent = kernel_call(
        functools.partial(back_kernel, per, False), "combine_grad", (flat, flat), *dr, info, after=(dots,)
    )
    grad_tokens = (kept + shift(sent, "exp", 1)).astype(BF16)
    return (mixed, grad_tokens, grad_probs, grad_gate[None], grad_up[None], grad_down[None])


def solution(mesh):
    sizes = dict(mesh.shape)
    fast = sizes["rep"] == 4 and sizes["exp"] == 8
    return jax.shard_map(
        on_quad if fast else on_device,
        mesh=mesh,
        in_specs=(
            P("exp", "rep"),
            P("exp", None),
            P("exp", None),
            P(),
            P(),
            P("exp", "rep"),
            P("exp", None, "rep"),
            P("exp", None, "rep"),
            P("exp", "rep", None),
        ),
        out_specs=(
            P("exp", "rep"),
            P("exp", "rep"),
            P("exp", None),
            P("exp", None, "rep"),
            P("exp", None, "rep"),
            P("exp", "rep", None),
        ),
        check_vma=False,
    )
```

```python
import functools

import jax
import jax.numpy as jnp
from jax import lax
from jax.experimental import pallas as pl
from jax.experimental.pallas import tpu as pltpu
from jax.sharding import PartitionSpec as P

HOT = 4


def carried_in(value, axis, combine, identity):
    peers, mine = (lax.axis_size(axis), lax.axis_index(axis))
    everything = lax.all_gather(value, axis)
    start = jnp.broadcast_to(jnp.asarray(identity, value.dtype), value.shape)

    def step(k, before):
        reached = k < mine
        new = combine(before, everything[k])
        return jnp.where(reached, new, before)

    return lax.fori_loop(0, peers, step, start)


def fill_rows(shard, flat, rank, token_of, scale, experts, per_slot):
    picked = shard[token_of]
    if scale is not None:
        picked = (picked.astype(jnp.float32) * scale[:, None]).astype(jnp.bfloat16)
    empty = jnp.zeros((experts, per_slot, shard.shape[1]), jnp.bfloat16)
    return empty.at[flat, rank].set(picked)


def dispatch(shard, flat, rank, token_of, scale, experts, per_slot):
    buffer = fill_rows(shard, flat, rank, token_of, scale, experts, per_slot)
    received = lax.all_to_all(buffer, "exp", split_axis=0, concat_axis=0, tiled=True)
    narrow = received.reshape(-1, received.shape[2])
    return lax.all_gather(narrow, "rep", axis=1, tiled=True)


def return_rows(rows, flat, rank, experts, per_slot):
    back = lax.all_to_all(
        rows.reshape(experts, per_slot, rows.shape[1]),
        "exp",
        split_axis=0,
        concat_axis=0,
        tiled=True,
    )
    return back[flat, rank].astype(jnp.float32)


def on_device(tokens, routes, probs, capacity, plan, grad_out, w_gate, w_up, w_down):
    tok_rows = tokens.shape[0]
    experts = capacity.shape[0]
    per_slot = 4 * tok_rows // experts
    feat_cols = tokens.shape[1]
    flat = routes.reshape(-1)
    expert_ids = jnp.arange(experts, dtype=jnp.int32)
    onehot = (flat[:, None] == expert_ids[None, :]).astype(jnp.int32)
    rank = jnp.sum((jnp.cumsum(onehot, axis=0) - onehot) * onehot, axis=1)
    counts = jnp.sum(onehot, axis=0)
    earlier = carried_in(
        counts, "exp", lambda first, second: first + second, jnp.zeros_like(counts)
    )
    position = rank + jnp.sum(onehot * earlier[None, :], axis=1)
    hot_flag = jnp.any(plan[:HOT][:, None] == expert_ids[None, :], axis=0).astype(jnp.int32)
    limit = capacity + 2 * tok_rows * hot_flag
    keep = (position < jnp.sum(onehot * limit[None, :], axis=1)).astype(jnp.float32)
    weight = probs.reshape(-1) * keep
    token_of = jnp.arange(2 * tok_rows, dtype=jnp.int32) // 2
    wg = w_gate[0]
    wu = w_up[0]
    wd = w_down[0]
    xs = dispatch(tokens, flat, rank, token_of, None, experts, per_slot)
    gate = jnp.dot(xs, wg, preferred_element_type=jnp.float32)
    up = jnp.dot(xs, wu, preferred_element_type=jnp.float32)
    sig = jax.nn.sigmoid(gate)
    silu = gate * sig
    hidden = (silu * up).astype(jnp.bfloat16)
    partial_value = jnp.dot(hidden, wd, preferred_element_type=jnp.float32)
    out_rows = lax.psum_scatter(
        partial_value.astype(jnp.bfloat16), "rep", scatter_dimension=1, tiled=True
    )
    picked = return_rows(out_rows, flat, rank, experts, per_slot)
    mixed = jnp.sum((weight[:, None] * picked).reshape(tok_rows, 2, feat_cols), axis=1).astype(
        jnp.bfloat16
    )
    dots = jnp.sum(grad_out[token_of].astype(jnp.float32) * picked, axis=1)
    dots = lax.psum(dots, "rep")
    grad_probs = (keep * dots).reshape(tok_rows, 2)
    dout = dispatch(grad_out, flat, rank, token_of, weight, experts, per_slot)
    dh = lax.dot_general(dout, wd, (((1,), (1,)), ((), ())), preferred_element_type=jnp.float32)
    dgate = (dh * up * sig * (1.0 + gate * (1.0 - sig))).astype(jnp.bfloat16)
    dup = (dh * silu).astype(jnp.bfloat16)
    grad_down = lax.dot_general(
        hidden, dout, (((0,), (0,)), ((), ())), preferred_element_type=jnp.float32
    )
    grad_gate = lax.dot_general(
        xs, dgate, (((0,), (0,)), ((), ())), preferred_element_type=jnp.float32
    )
    grad_up = lax.dot_general(xs, dup, (((0,), (0,)), ((), ())), preferred_element_type=jnp.float32)
    dpartial = lax.dot_general(
        dgate, wg, (((1,), (1,)), ((), ())), preferred_element_type=jnp.float32
    )
    dpartial = dpartial + lax.dot_general(
        dup, wu, (((1,), (1,)), ((), ())), preferred_element_type=jnp.float32
    )
    dx_rows = lax.psum_scatter(
        dpartial.astype(jnp.bfloat16), "rep", scatter_dimension=1, tiled=True
    )
    back = return_rows(dx_rows, flat, rank, experts, per_slot)
    grad_tokens = jnp.sum((weight[:, None] * back).reshape(tok_rows, 2, feat_cols), axis=1).astype(
        jnp.bfloat16
    )
    return (mixed, grad_tokens, grad_probs, grad_gate[None], grad_up[None], grad_down[None])


F32 = jnp.float32
BF16 = jnp.bfloat16
I32 = jnp.int32
CHIPS = 4
VMEM_BYTES = 14 * 1024 * 1024


def dot(a, b, dims=((1,), (0,))):
    return lax.dot_general(a, b, (dims, ((), ())), preferred_element_type=F32)


def params(**kw):
    return pltpu.CompilerParams(vmem_limit_bytes=VMEM_BYTES, **kw)


def vmem():
    return pl.BlockSpec(memory_space=pltpu.VMEM)


def smem():
    return pl.BlockSpec(memory_space=pltpu.SMEM)


def table_of(routes, probs):
    return jnp.concatenate([routes[...].astype(F32), probs[...]], axis=0)


def place_rows(ids, own, par, per):
    z, c = ids[0], ids[1]
    toks = own.shape[1]
    row = lax.broadcasted_iota(I32, (2 * CHIPS, toks), 0)
    expert = 2 * (z ^ (row % CHIPS)) + c
    first = row < CHIPS
    named = [
        jnp.where(first, own[k : k + 1, :], par[k : k + 1, :]).astype(I32) == expert
        for k in range(2)
    ]
    either = jnp.logical_or(named[0], named[1])
    before = lax.broadcasted_iota(I32, (toks, toks), 0) < lax.broadcasted_iota(
        I32, (toks, toks), 1
    )
    rank = dot(either.astype(F32).astype(BF16), before.astype(F32).astype(BF16)).astype(I32)
    return row, expert, named, either, rank


def pick(rank, either, i, per):
    at = jnp.where(either[i : i + 1, :], rank[i : i + 1, :], -1)
    slots = lax.broadcasted_iota(I32, (per, at.shape[1]), 0)
    return (slots == at).astype(F32)


def thirds(line):
    high = line.astype(BF16).astype(F32)
    middle = (line - high).astype(BF16).astype(F32)
    return high, middle, line - high - middle


def send_kernel(per, ids, own_x, own_g, own_r, own_p, par_r, par_p, par_x, par_g, c0, c1, c2, c3):
    own, par = table_of(own_r, own_p), table_of(par_r, par_p)
    toks = own.shape[1]
    feats = own_x.shape[1]
    _, _, _, either, rank = place_rows(ids, own, par, per)
    tail = lax.broadcasted_iota(I32, (16, toks), 0)
    lines = [own[0:1, :], own[1:2, :], par[0:1, :], par[1:2, :]]
    for table in (own, par):
        for k in range(2):
            lines += thirds(table[2 + k : 3 + k, :])
    extra = jnp.zeros((16, toks), F32)
    for i, line in enumerate(lines):
        extra = jnp.where(tail == i, line, extra)
    for q, out in enumerate((c0, c1, c2, c3)):
        for src in range(2):
            hot = pick(rank, either, CHIPS * src + q, per).astype(BF16)
            place = slice(src * per, (src + 1) * per)
            out[place, 0:feats] = dot(hot, (own_x, par_x)[src][...]).astype(BF16)
            out[place, feats : 2 * feats] = dot(hot, (own_g, par_g)[src][...]).astype(BF16)
        if q:
            out[2 * per : 2 * per + 16, 0:toks] = extra.astype(BF16)
            out[2 * per : 2 * per + 16, toks : 2 * toks] = jnp.zeros((16, toks), BF16)


def room_of(e, cap, plan, extra_slots):
    room = cap[e]
    for h in range(HOT):
        room = room + jnp.where(plan[h] == e, extra_slots, 0)
    return room


def place_kernel(per, extra_slots, ids, cap, plan, own_r, own_p, par_r, par_p, e1, e2, e3, info, near_scale, far_scale):
    own, par = table_of(own_r, own_p), table_of(par_r, par_p)
    toks = own.shape[1]
    z, c = ids[0], ids[1]
    row, expert, named, either, rank = place_rows(ids, own, par, per)
    q_col = row[:, 0:1] % CHIPS
    first = row < CHIPS
    first_col = first[:, 0:1]

    sources = []
    for s, table in enumerate((own, par)):
        sources.append((0, s, [table[k : k + 1, :] for k in range(4)]))
    for p, ref in ((1, e1), (2, e2), (3, e3)):
        table = ref[2 * per : 2 * per + 16, 0:toks].astype(F32)
        for s in range(2):
            lines = [table[2 * s + k : 2 * s + k + 1, :] for k in range(2)]
            for k in range(2):
                at = 4 + 3 * (2 * s + k)
                lines.append(
                    table[at : at + 1, :] + table[at + 1 : at + 2, :] + table[at + 2 : at + 3, :]
                )
            sources.append((p, s, lines))

    limit = jnp.zeros((2 * CHIPS, 1), I32)
    for q in range(CHIPS):
        limit = jnp.where(q_col == q, room_of(2 * (z ^ q) + c, cap, plan, extra_slots), limit)
    earlier = jnp.zeros((2 * CHIPS, 1), F32)
    for p, s, lines in sources:
        hits = jnp.logical_or(lines[0].astype(I32) == expert, lines[1].astype(I32) == expert)
        count = jnp.sum(hits.astype(F32), axis=1, keepdims=True)
        block = 2 * (z ^ p) + (c ^ s)
        ahead = jnp.where(
            first_col,
            (block < 2 * z + c).astype(F32),
            (block < 2 * z + (c ^ 1)).astype(F32),
        )
        earlier = earlier + count * ahead
    keep = jnp.where(rank + earlier.astype(I32) < limit, 1.0, 0.0)
    kinds = []
    for k in range(2):
        prob = jnp.where(first, own[2 + k : 3 + k, :], par[2 + k : 3 + k, :])
        mine = named[k].astype(F32)
        slot = (row % CHIPS * per + rank + 1).astype(F32)
        kinds.append((mine * slot, mine * keep * prob, mine * keep))
    at = lax.broadcasted_iota(I32, (128, toks), 0)
    table = jnp.zeros((128, toks), F32)
    for kind in range(3):
        for src in range(2):
            half = first if src == 0 else jnp.logical_not(first)
            for k in range(2):
                line = jnp.sum(jnp.where(half, kinds[k][kind], 0.0), axis=0, keepdims=True)
                table = jnp.where(at == 4 * kind + 2 * src + k, line, table)
    info[...] = jnp.transpose(table)

    stacked = [jnp.zeros((2 * CHIPS, toks), F32) for _ in range(4)]
    blocks = jnp.zeros((2 * CHIPS, 1), I32)
    for p, s, lines in sources:
        i = 2 * p + s
        stacked = [jnp.where(row == i, line, old) for line, old in zip(lines, stacked)]
        blocks = jnp.where(row[:, 0:1] == i, 2 * (z ^ p) + (c ^ s), blocks)
    mine = 2 * z + c
    named = [stacked[k].astype(I32) == mine for k in range(2)]
    either = jnp.logical_or(named[0], named[1])
    before = lax.broadcasted_iota(I32, (toks, toks), 0) < lax.broadcasted_iota(
        I32, (toks, toks), 1
    )
    hits = either.astype(F32)
    rank = dot(hits.astype(BF16), before.astype(F32).astype(BF16)).astype(I32)
    count = jnp.sum(hits, axis=1, keepdims=True)
    earlier = jnp.zeros((2 * CHIPS, 1), F32)
    for p, s, _ in sources:
        i = 2 * p + s
        ahead = (2 * (z ^ p) + (c ^ s) < blocks).astype(F32)
        earlier = earlier + ahead * count[i : i + 1, :]
    keep = rank + earlier.astype(I32) < room_of(mine, cap, plan, extra_slots)
    weight = jnp.where(keep, 1.0, 0.0) * (
        named[0].astype(F32) * stacked[2] + named[1].astype(F32) * stacked[3]
    )
    for i in range(2 * CHIPS):
        hot = pick(rank, either, i, per)
        value = jnp.sum(hot * weight[i : i + 1, :], axis=1, keepdims=True)
        at = i % 4 * per
        (near_scale, far_scale)[i // 4][at : at + per, :] = jnp.broadcast_to(value, (per, 128))


def load_kernel(a, b, c, after, x, y, z, sems):
    copies = [
        pltpu.make_async_copy(src, dst, sems.at[i])
        for i, (src, dst) in enumerate(((a, x), (b, y), (c, z)))
    ]
    for copy in copies:
        copy.start()
    for copy in copies:
        copy.wait()


def combine(per, src, k, rows, info):
    slot = info[:, 2 * src + k : 2 * src + k + 1].astype(I32) - 1
    slots = lax.broadcasted_iota(I32, (info.shape[0], CHIPS * per), 1)
    return dot((slots == slot).astype(F32).astype(BF16), rows)


def back_kernel(per, with_dots, at0, feats, y0, y1, y2, y3, info_ref, *refs):
    if with_dots:
        own_g, par_g, kept, sent, kept_dots, sent_dots = refs
    else:
        kept, sent = refs
    info = info_ref[...]
    toks = info.shape[0]
    starts = [at0 if y.shape[1] > feats else 0 for y in (y0, y1, y2, y3)]
    lane = lax.broadcasted_iota(I32, (toks, 128), 1)
    for src, out in enumerate((kept, sent)):
        rows = jnp.concatenate(
            [
                y[src * per : (src + 1) * per, at : at + feats]
                for y, at in zip((y0, y1, y2, y3), starts)
            ],
            axis=0,
        )
        total = jnp.zeros((toks, feats), F32)
        dots = jnp.zeros((toks, 128), F32)
        for k in range(2):
            picked = combine(per, src, k, rows, info)
            at = 2 * src + k
            total = total + info[:, 4 + at : 5 + at] * picked
            if with_dots:
                grad = (own_g, par_g)[src][...].astype(F32)
                inner = jnp.sum(grad * picked, axis=1, keepdims=True) * info[:, 8 + at : 9 + at]
                dots = jnp.where(lane == k, inner, dots)
        out[...] = total.astype(out.dtype)
        if with_dots:
            (kept_dots, sent_dots)[src][...] = jnp.transpose(dots)[0:8, :]


def assemble(r, shards, at, feats, cat, scale):
    own, a, b, c, d = shards
    rows = own.shape[0]
    half = rows // 2
    lanes = slice(at, at + feats)
    factor = None if scale is None else scale[:, 0:1]
    for k, start, ref in ((0, 0, own), (1, 0, a), (2, 0, b), (3, 0, c), (3, half, d)):
        cols = pl.ds(pl.multiple_of((r ^ k) * feats, feats), feats)
        size = ref.shape[0]
        piece = ref[:, lanes]
        if factor is not None:
            piece = (piece.astype(F32) * factor[start : start + size, :]).astype(BF16)
        cat[start : start + size, cols] = piece


def split_out(part, outs, feats, low, high):
    send_a, keep_a, send_b, keep_b = outs
    half = send_a.shape[0]
    low, high = slice(low, low + feats), slice(high, high + feats)
    for k in (3, 1, 2, 0):
        piece = part(k).astype(BF16)
        top = ((keep_a, low), (send_a, low), (keep_a, high), (send_a, high))[k]
        bottom = ((keep_b, low), (keep_b, high), (send_b, low), (send_b, high))[k]
        top[0][:, top[1]] = piece[0:half, :]
        bottom[0][:, bottom[1]] = piece[half : 2 * half, :]


def forward(r, shards, wg, wu, wd, cat, hid, act, slope, outs, low, high):
    feats = shards[0].shape[1] // 2
    assemble(r, shards, 0, feats, cat, None)
    step = 256
    for j in range(0, hid.shape[1], step):
        cols = slice(j, j + step)
        gate = dot(cat[...], wg[:, cols])
        up = dot(cat[...], wu[:, cols])
        sig = jax.nn.sigmoid(gate)
        silu = gate * sig
        hid[:, cols] = (silu * up).astype(BF16)
        act[:, cols] = silu.astype(act.dtype)
        slope[:, cols] = (up * (sig + silu * (1.0 - sig))).astype(slope.dtype)

    def part(k):
        return dot(hid[...], wd[:, pl.ds(pl.multiple_of((r ^ k) * feats, feats), feats)])

    split_out(part, outs, feats, low, high)


def backward(r, shards, scale, wg, wu, wd, act, slope, cat, dgate, dup, outs, low, high):
    feats = shards[0].shape[1] // 2
    assemble(r, shards, feats, feats, cat, scale)
    step = 256
    for j in range(0, dgate.shape[1], step):
        cols = slice(j, j + step)
        dh = dot(cat[...], wd[cols, :], ((1,), (1,)))
        dgate[:, cols] = (dh * slope[:, cols].astype(F32)).astype(BF16)
        dup[:, cols] = (dh * act[:, cols].astype(F32)).astype(BF16)

    def part(k):
        line = pl.ds(pl.multiple_of((r ^ k) * feats, feats), feats)
        return dot(dgate[...], wg[line, :], ((1,), (1,))) + dot(dup[...], wu[line, :], ((1,), (1,)))

    split_out(part, outs, feats, low, high)


def near_kernel(ids, *refs):
    shards, (scale, wg, wu, wd), refs = refs[:5], refs[5:9], refs[9:]
    (xcat, hid, gcat, dgate, dup), outs, (act, slope) = refs[:5], refs[5:9], refs[9:]
    r, feats = ids[2], shards[0].shape[1] // 2
    forward(r, shards, wg, wu, wd, xcat, hid, act, slope, outs, 0, 2 * feats)
    backward(r, shards, scale, wg, wu, wd, act, slope, gcat, dgate, dup, outs, feats, 3 * feats)


def far_forward_kernel(ids, *refs):
    shards, (wg, wu, wd), (xcat, hid, act, slope), outs = refs[:5], refs[5:8], refs[8:12], refs[12:]
    feats = shards[0].shape[1] // 2
    forward(ids[2], shards, wg, wu, wd, xcat, hid, act, slope, outs, 0, feats)


def far_backward_kernel(ids, *refs):
    shards, (scale, wg, wu, wd, act, slope) = refs[:5], refs[5:11]
    (gcat, dgate, dup), outs = refs[11:14], refs[14:]
    feats = shards[0].shape[1] // 2
    backward(ids[2], shards, scale, wg, wu, wd, act, slope, gcat, dgate, dup, outs, 0, feats)


def weights_kernel(left_a, left_b, right_a, right_b, after, out, done):
    done[...] = jnp.zeros_like(done)
    size = out.shape[0]
    cols = pl.ds(pl.multiple_of(pl.program_id(0) * size, size), size)
    out[...] = dot(left_a[:, cols], right_a[...], ((0,), (0,))) + dot(
        left_b[:, cols], right_b[...], ((0,), (0,))
    )


def join_kernel(a, b, out):
    size = out.shape[0] // 2
    out[0:size, :] = a[0:size, :]
    out[size : 2 * size, :] = b[0:size, :]


def middle_kernel(ka, ra, kb, rb, sa, sb, kept):
    half, feats = sa.shape
    kept[0:half, :] = ka[:, 0:feats].astype(F32) + ra[:, 0:feats].astype(F32)
    kept[half : 2 * half, :] = kb[:, 0:feats].astype(F32) + rb[:, 0:feats].astype(F32)
    sa[...] = (ka[:, feats:].astype(F32) + ra[:, feats:].astype(F32)).astype(BF16)
    sb[...] = (kb[:, feats:].astype(F32) + rb[:, feats:].astype(F32)).astype(BF16)


def last_kernel(kept, ra, rb, *outs):
    half = ra.shape[0]
    size = outs[0].shape[0]
    for q, out in enumerate(outs):
        at = q * size
        other = ra[at : at + size, :] if at < half else rb[at - half : at - half + size, :]
        out[...] = (kept[at : at + size, :] + other.astype(F32)).astype(BF16)


def shift(x, axis, bit):
    n = lax.axis_size(axis)
    return lax.ppermute(x, axis, [(i, i ^ bit) for i in range(n)])


def sds(shape, dtype):
    return jax.ShapeDtypeStruct(shape, dtype)


def vm(shape, dtype):
    return pltpu.VMEM(shape, dtype)


def pin(*arrays):
    return [pltpu.with_memory_space_constraint(x, pltpu.VMEM) for x in arrays]


def grad_kernel(per, feats, y0, y1, y2, y3, info, dots, kept, sent, dots_out):
    back_kernel(per, False, feats, feats, y0, y1, y2, y3, info, kept, sent)
    dots_out[...] = dots[...]


def kernel_call(body, name, outs, *args, plan_args=0, loose=0, flops=1, after=(), scratch=()):
    count = len(args)
    pinned = list(args[:plan_args])
    for x in args[plan_args : plan_args + loose]:
        pinned.append(pltpu.with_memory_space_constraint(x, pltpu.HBM))
    pinned += pin(*args[plan_args + loose :], *after)

    def run(*refs):
        body(*refs[:count], *refs[count + len(after) :])

    return pl.pallas_call(
        run,
        in_specs=[smem()] * plan_args + [vmem()] * (count - plan_args + len(after)),
        out_shape=outs,
        scratch_shapes=scratch,
        compiler_params=params(),
        cost_estimate=pl.CostEstimate(flops=flops, bytes_accessed=1 << 20, transcendentals=0),
        name=name,
    )(*pinned)


def relay_kernel(a, b, top, bottom):
    half = top.shape[0]
    top[...] = a[0:half, :]
    bottom[...] = b[half : 2 * half, :]


def gather_first(x):
    return x, shift(x, "rep", 1), shift(x, "rep", 2)


def gather_second(parts, after):
    x, a, b = parts
    half = vm((x.shape[0] // 2, x.shape[1]), BF16)
    top, bottom = kernel_call(relay_kernel, "relay", (half, half), a, b, after=after)
    return x, a, b, shift(top, "rep", 2), shift(bottom, "rep", 1)


def reduce_first(sa, ka, sb, kb):
    return ka, shift(sa, "rep", 1), kb, shift(sb, "rep", 2)


def reduce_second(parts, after=()):
    half, feats = parts[0].shape[0], parts[0].shape[1] // 2
    piece = vm((half, feats), BF16)
    ma, mb, kept = kernel_call(
        middle_kernel, "reduce_middle", (piece, piece, vm((2 * half, feats), F32)), *parts, after=after
    )
    return kept, shift(ma, "rep", 2), shift(mb, "rep", 1)


def reduce_last(parts, size, after=()):
    rows, feats = parts[0].shape
    outs = (vm((size, feats), BF16),) * (rows // size)
    return kernel_call(last_kernel, "reduce_last", outs, *parts, after=after)


def over_chips(chunks):
    return over_chips_from(0, chunks)


def over_chips_from(first, chunks):
    return [c if first + n == 0 else shift(c, "exp", 2 * (first + n)) for n, c in enumerate(chunks)]


def on_quad(tokens, routes, probs, capacity, plan, grad_out, w_gate, w_up, w_down):
    toks, feats = tokens.shape
    per = 4 * toks // capacity.shape[0]
    wg, wu, wd = w_gate[0], w_up[0], w_down[0]
    width, ff = wg.shape
    rows = 2 * per * CHIPS
    me = lax.axis_index("exp").astype(I32)
    ids = jnp.stack([me // 2, me % 2, lax.axis_index("rep").astype(I32)])
    own_m = (routes.T, probs.T)
    par_m = tuple(shift(x, "exp", 1) for x in own_m)
    par_x = shift(tokens, "exp", 1)
    par_g = shift(grad_out, "exp", 1)

    size = 2 * per
    both = 2 * feats
    stay = vm((size, both), BF16)
    go = vm((size + 16, both), BF16)
    sent = kernel_call(
        functools.partial(send_kernel, per),
        "send",
        (stay, go, go, go),
        ids, tokens, grad_out, *own_m, *par_m, par_x, par_g,
        plan_args=1,
        loose=2,
    )
    got = over_chips(sent)
    pair_rows = vm((2 * size, both), BF16)
    near = gather_first(kernel_call(join_kernel, "join_near", pair_rows, got[0], got[1]))
    loaded = vm((width, ff), BF16)
    wg, wu, wd = pl.pallas_call(
        load_kernel,
        in_specs=[pl.BlockSpec(memory_space=pltpu.HBM)] * 3 + [vmem()],
        out_shape=(loaded, loaded, vm((ff, width), BF16)),
        scratch_shapes=[pltpu.SemaphoreType.DMA((3,))],
        compiler_params=params(),
        cost_estimate=pl.CostEstimate(flops=2*10**10, bytes_accessed=24 << 20, transcendentals=0),
        name="load_weights",
    )(*[pltpu.with_memory_space_constraint(w, pltpu.HBM) for w in (wg, wu, wd)], *pin(near[0]))
    far = gather_first(
        kernel_call(join_kernel, "join_far", pair_rows, got[2], got[3], after=(wg,))
    )
    info, near_scale, far_scale = kernel_call(
        functools.partial(place_kernel, per, 2 * toks),
        "place",
        (vm((toks, 128), F32), vm((2 * size, 128), F32), vm((2 * size, 128), F32)),
        ids, capacity, plan, *own_m, *par_m, *got[1:],
        plan_args=3,
    )
    near = gather_second(near, (far[0],))

    inner = vm((2 * size, ff), BF16)
    wide = vm((2 * size, width), BF16)
    work = 2 * (2 * size) * width * ff
    near_x, near_hid, near_g, near_dgate, near_dup, *near_parts = kernel_call(
        near_kernel,
        "near",
        (wide, inner, wide, inner, inner) + (vm((size, 2 * both), BF16),) * 4,
        ids, *near, near_scale, wg, wu, wd,
        plan_args=1,
        flops=6 * work,
        scratch=[pltpu.VMEM((2 * size, ff), F32)] * 2,
    )
    far = gather_second(far, (near_hid,))
    near_first = reduce_first(*near_parts)
    part = vm((size, both), BF16)
    far_x, far_hid, act, slope, *out_parts = kernel_call(
        far_forward_kernel,
        "far_forward",
        (wide, inner, inner, inner) + (part,) * 4,
        ids, *far, wg, wu, wd,
        plan_args=1,
        flops=3 * work,
    )
    out_first = reduce_first(*out_parts)
    far_g, far_dgate, far_dup, *dx_parts = kernel_call(
        far_backward_kernel,
        "far_backward",
        (wide, inner, inner) + (part,) * 4,
        ids, *far, far_scale, wg, wu, wd, act, slope,
        plan_args=1,
        flops=3 * work,
        after=out_parts[:1],
    )
    dx_first = reduce_first(*dx_parts)

    def weight_grad(name, left, right, n, m, after):
        steps = 4
        return pl.pallas_call(
            weights_kernel,
            grid=(steps,),
            in_specs=[vmem()] * 5,
            out_specs=[pl.BlockSpec((n // steps, m), lambda i: (i, 0)), vmem()],
            out_shape=(sds((n, m), F32), vm((8, 128), F32)),
            compiler_params=params(),
            cost_estimate=pl.CostEstimate(flops=2*10**10, bytes_accessed=1, transcendentals=0),
            name=name,
        )(*pin(*left, *right, after))

    near_sums = reduce_second(near_first, (far_dgate,))
    out_sums = reduce_second(out_first, (near_sums[0],))
    grad_down, done_d = weight_grad(
        "grad_down", (near_hid, far_hid), (near_g, far_g), ff, width, out_sums[0]
    )
    dx_sums = reduce_second(dx_first, (done_d,))
    out_rows = reduce_last(out_sums, size, (dx_sums[0],))
    back_out = over_chips_from(2, out_rows)
    grad_gate, done_g = weight_grad(
        "grad_gate", (near_x, far_x), (near_dgate, far_dgate), width, ff, out_rows[0]
    )
    dx_rows = reduce_last(dx_sums, size, (done_g,))
    back_dx = over_chips_from(2, dx_rows)
    near_rows = reduce_last(near_sums, size, dx_rows[:1])
    back_near = over_chips_from(0, near_rows)
    grad_up, done_u = weight_grad(
        "grad_up", (near_x, far_x), (near_dup, far_dup), width, ff, near_rows[0]
    )

    whole, narrow, few = vm((toks, feats), F32), vm((toks, feats), BF16), vm((8, toks), F32)
    kept, sent, kept_dots, sent_dots = kernel_call(
        functools.partial(back_kernel, per, True, 0, feats),
        "combine_out",
        (whole, narrow, few, few),
        *back_near, *back_out, info, grad_out, par_g,
        after=(done_u,),
    )
    mixed = (kept + shift(sent, "exp", 1).astype(F32)).astype(BF16)
    dots = kept_dots + shift(sent_dots, "exp", 1)
    kept, sent, dots = kernel_call(
        functools.partial(grad_kernel, per, feats),
        "combine_grad",
        (whole, narrow, few),
        *back_near, *back_dx, info, dots,
    )
    first = dots[0:2]
    second, third, fourth = (shift(first, "rep", k) for k in (1, 2, 3))
    grad_probs = ((first + second) + (third + fourth)).T
    grad_tokens = (kept + shift(sent, "exp", 1).astype(F32)).astype(BF16)
    return (mixed, grad_tokens, grad_probs, grad_gate[None], grad_up[None], grad_down[None])


def solution(mesh):
    sizes = dict(mesh.shape)
    fast = sizes["rep"] == 4 and sizes["exp"] == 8
    return jax.shard_map(
        on_quad if fast else on_device,
        mesh=mesh,
        in_specs=(
            P("exp", "rep"),
            P("exp", None),
            P("exp", None),
            P(),
            P(),
            P("exp", "rep"),
            P("exp", None, "rep"),
            P("exp", None, "rep"),
            P("exp", "rep", None),
        ),
        out_specs=(
            P("exp", "rep"),
            P("exp", "rep"),
            P("exp", None),
            P("exp", None, "rep"),
            P("exp", None, "rep"),
            P("exp", "rep", None),
        ),
        check_vma=False,
    )
```

```python
import functools

import jax
import jax.numpy as jnp
from jax import lax
from jax.experimental import pallas as pl
from jax.experimental.pallas import tpu as pltpu
from jax.sharding import PartitionSpec as P

HOT = 4


def carried_in(value, axis, combine, identity):
    peers, mine = (lax.axis_size(axis), lax.axis_index(axis))
    everything = lax.all_gather(value, axis)
    start = jnp.broadcast_to(jnp.asarray(identity, value.dtype), value.shape)

    def step(k, before):
        reached = k < mine
        new = combine(before, everything[k])
        return jnp.where(reached, new, before)

    return lax.fori_loop(0, peers, step, start)


def fill_rows(shard, flat, rank, token_of, scale, experts, per_slot):
    picked = shard[token_of]
    if scale is not None:
        picked = (picked.astype(jnp.float32) * scale[:, None]).astype(jnp.bfloat16)
    empty = jnp.zeros((experts, per_slot, shard.shape[1]), jnp.bfloat16)
    return empty.at[flat, rank].set(picked)


def dispatch(shard, flat, rank, token_of, scale, experts, per_slot):
    buffer = fill_rows(shard, flat, rank, token_of, scale, experts, per_slot)
    received = lax.all_to_all(buffer, "exp", split_axis=0, concat_axis=0, tiled=True)
    narrow = received.reshape(-1, received.shape[2])
    return lax.all_gather(narrow, "rep", axis=1, tiled=True)


def return_rows(rows, flat, rank, experts, per_slot):
    back = lax.all_to_all(
        rows.reshape(experts, per_slot, rows.shape[1]),
        "exp",
        split_axis=0,
        concat_axis=0,
        tiled=True,
    )
    return back[flat, rank].astype(jnp.float32)


def on_device(tokens, routes, probs, capacity, plan, grad_out, w_gate, w_up, w_down):
    tok_rows = tokens.shape[0]
    experts = capacity.shape[0]
    per_slot = 4 * tok_rows // experts
    feat_cols = tokens.shape[1]
    flat = routes.reshape(-1)
    expert_ids = jnp.arange(experts, dtype=jnp.int32)
    onehot = (flat[:, None] == expert_ids[None, :]).astype(jnp.int32)
    rank = jnp.sum((jnp.cumsum(onehot, axis=0) - onehot) * onehot, axis=1)
    counts = jnp.sum(onehot, axis=0)
    earlier = carried_in(
        counts, "exp", lambda first, second: first + second, jnp.zeros_like(counts)
    )
    position = rank + jnp.sum(onehot * earlier[None, :], axis=1)
    hot_flag = jnp.any(plan[:HOT][:, None] == expert_ids[None, :], axis=0).astype(jnp.int32)
    limit = capacity + 2 * tok_rows * hot_flag
    keep = (position < jnp.sum(onehot * limit[None, :], axis=1)).astype(jnp.float32)
    weight = probs.reshape(-1) * keep
    token_of = jnp.arange(2 * tok_rows, dtype=jnp.int32) // 2
    wg = w_gate[0]
    wu = w_up[0]
    wd = w_down[0]
    xs = dispatch(tokens, flat, rank, token_of, None, experts, per_slot)
    gate = jnp.dot(xs, wg, preferred_element_type=jnp.float32)
    up = jnp.dot(xs, wu, preferred_element_type=jnp.float32)
    sig = jax.nn.sigmoid(gate)
    silu = gate * sig
    hidden = (silu * up).astype(jnp.bfloat16)
    partial_value = jnp.dot(hidden, wd, preferred_element_type=jnp.float32)
    out_rows = lax.psum_scatter(
        partial_value.astype(jnp.bfloat16), "rep", scatter_dimension=1, tiled=True
    )
    picked = return_rows(out_rows, flat, rank, experts, per_slot)
    mixed = jnp.sum((weight[:, None] * picked).reshape(tok_rows, 2, feat_cols), axis=1).astype(
        jnp.bfloat16
    )
    dots = jnp.sum(grad_out[token_of].astype(jnp.float32) * picked, axis=1)
    dots = lax.psum(dots, "rep")
    grad_probs = (keep * dots).reshape(tok_rows, 2)
    dout = dispatch(grad_out, flat, rank, token_of, weight, experts, per_slot)
    dh = lax.dot_general(dout, wd, (((1,), (1,)), ((), ())), preferred_element_type=jnp.float32)
    dgate = (dh * up * sig * (1.0 + gate * (1.0 - sig))).astype(jnp.bfloat16)
    dup = (dh * silu).astype(jnp.bfloat16)
    grad_down = lax.dot_general(
        hidden, dout, (((0,), (0,)), ((), ())), preferred_element_type=jnp.float32
    )
    grad_gate = lax.dot_general(
        xs, dgate, (((0,), (0,)), ((), ())), preferred_element_type=jnp.float32
    )
    grad_up = lax.dot_general(xs, dup, (((0,), (0,)), ((), ())), preferred_element_type=jnp.float32)
    dpartial = lax.dot_general(
        dgate, wg, (((1,), (1,)), ((), ())), preferred_element_type=jnp.float32
    )
    dpartial = dpartial + lax.dot_general(
        dup, wu, (((1,), (1,)), ((), ())), preferred_element_type=jnp.float32
    )
    dx_rows = lax.psum_scatter(
        dpartial.astype(jnp.bfloat16), "rep", scatter_dimension=1, tiled=True
    )
    back = return_rows(dx_rows, flat, rank, experts, per_slot)
    grad_tokens = jnp.sum((weight[:, None] * back).reshape(tok_rows, 2, feat_cols), axis=1).astype(
        jnp.bfloat16
    )
    return (mixed, grad_tokens, grad_probs, grad_gate[None], grad_up[None], grad_down[None])


F32 = jnp.float32
BF16 = jnp.bfloat16
I32 = jnp.int32
CHIPS = 4
VMEM_BYTES = 14 * 1024 * 1024


def dot(a, b, dims=((1,), (0,))):
    return lax.dot_general(a, b, (dims, ((), ())), preferred_element_type=F32)


def params(**kw):
    return pltpu.CompilerParams(vmem_limit_bytes=VMEM_BYTES, **kw)


def vmem():
    return pl.BlockSpec(memory_space=pltpu.VMEM)


def smem():
    return pl.BlockSpec(memory_space=pltpu.SMEM)


def table_of(routes, probs):
    return jnp.concatenate([routes[...].astype(F32), probs[...]], axis=0)


def place_rows(ids, own, par, per):
    z, c = ids[0], ids[1]
    toks = own.shape[1]
    row = lax.broadcasted_iota(I32, (2 * CHIPS, toks), 0)
    expert = 2 * (z ^ (row % CHIPS)) + c
    first = row < CHIPS
    named = [
        jnp.where(first, own[k : k + 1, :], par[k : k + 1, :]).astype(I32) == expert
        for k in range(2)
    ]
    either = jnp.logical_or(named[0], named[1])
    before = lax.broadcasted_iota(I32, (toks, toks), 0) < lax.broadcasted_iota(
        I32, (toks, toks), 1
    )
    rank = dot(either.astype(F32).astype(BF16), before.astype(F32).astype(BF16)).astype(I32)
    return row, expert, named, either, rank


def pick(rank, either, i, per):
    at = jnp.where(either[i : i + 1, :], rank[i : i + 1, :], -1)
    slots = lax.broadcasted_iota(I32, (per, at.shape[1]), 0)
    return (slots == at).astype(F32)


def thirds(line):
    high = line.astype(BF16).astype(F32)
    middle = (line - high).astype(BF16).astype(F32)
    return high, middle, line - high - middle


def send_kernel(per, ids, own_x, own_g, own_r, own_p, par_r, par_p, par_x, par_g, c0, c1, c2, c3):
    own, par = table_of(own_r, own_p), table_of(par_r, par_p)
    toks = own.shape[1]
    feats = own_x.shape[1]
    _, _, _, either, rank = place_rows(ids, own, par, per)
    tail = lax.broadcasted_iota(I32, (16, toks), 0)
    lines = [own[0:1, :], own[1:2, :], par[0:1, :], par[1:2, :]]
    for table in (own, par):
        for k in range(2):
            lines += thirds(table[2 + k : 3 + k, :])
    extra = jnp.zeros((16, toks), F32)
    for i, line in enumerate(lines):
        extra = jnp.where(tail == i, line, extra)
    for q, out in enumerate((c0, c1, c2, c3)):
        for src in range(2):
            hot = pick(rank, either, CHIPS * src + q, per).astype(BF16)
            place = slice(src * per, (src + 1) * per)
            out[place, 0:feats] = dot(hot, (own_x, par_x)[src][...]).astype(BF16)
            out[place, feats : 2 * feats] = dot(hot, (own_g, par_g)[src][...]).astype(BF16)
        if q:
            out[2 * per : 2 * per + 16, 0:toks] = extra.astype(BF16)
            out[2 * per : 2 * per + 16, toks : 2 * toks] = jnp.zeros((16, toks), BF16)


def room_of(e, cap, plan, extra_slots):
    room = cap[e]
    for h in range(HOT):
        room = room + jnp.where(plan[h] == e, extra_slots, 0)
    return room


def place_kernel(per, extra_slots, ids, cap, plan, own_r, own_p, par_r, par_p, e1, e2, e3, info, near_scale, far_scale):
    own, par = table_of(own_r, own_p), table_of(par_r, par_p)
    toks = own.shape[1]
    z, c = ids[0], ids[1]
    row, expert, named, either, rank = place_rows(ids, own, par, per)
    q_col = row[:, 0:1] % CHIPS
    first = row < CHIPS
    first_col = first[:, 0:1]

    sources = []
    for s, table in enumerate((own, par)):
        sources.append((0, s, [table[k : k + 1, :] for k in range(4)]))
    for p, ref in ((1, e1), (2, e2), (3, e3)):
        table = ref[2 * per : 2 * per + 16, 0:toks].astype(F32)
        for s in range(2):
            lines = [table[2 * s + k : 2 * s + k + 1, :] for k in range(2)]
            for k in range(2):
                at = 4 + 3 * (2 * s + k)
                lines.append(
                    table[at : at + 1, :] + table[at + 1 : at + 2, :] + table[at + 2 : at + 3, :]
                )
            sources.append((p, s, lines))

    limit = jnp.zeros((2 * CHIPS, 1), I32)
    for q in range(CHIPS):
        limit = jnp.where(q_col == q, room_of(2 * (z ^ q) + c, cap, plan, extra_slots), limit)
    earlier = jnp.zeros((2 * CHIPS, 1), F32)
    for p, s, lines in sources:
        hits = jnp.logical_or(lines[0].astype(I32) == expert, lines[1].astype(I32) == expert)
        count = jnp.sum(hits.astype(F32), axis=1, keepdims=True)
        block = 2 * (z ^ p) + (c ^ s)
        ahead = jnp.where(
            first_col,
            (block < 2 * z + c).astype(F32),
            (block < 2 * z + (c ^ 1)).astype(F32),
        )
        earlier = earlier + count * ahead
    keep = jnp.where(rank + earlier.astype(I32) < limit, 1.0, 0.0)
    kinds = []
    for k in range(2):
        prob = jnp.where(first, own[2 + k : 3 + k, :], par[2 + k : 3 + k, :])
        mine = named[k].astype(F32)
        slot = (row % CHIPS * per + rank + 1).astype(F32)
        kinds.append((mine * slot, mine * keep * prob, mine * keep))
    at = lax.broadcasted_iota(I32, (128, toks), 0)
    table = jnp.zeros((128, toks), F32)
    for kind in range(3):
        for src in range(2):
            half = first if src == 0 else jnp.logical_not(first)
            for k in range(2):
                line = jnp.sum(jnp.where(half, kinds[k][kind], 0.0), axis=0, keepdims=True)
                table = jnp.where(at == 4 * kind + 2 * src + k, line, table)
    info[...] = jnp.transpose(table)

    stacked = [jnp.zeros((2 * CHIPS, toks), F32) for _ in range(4)]
    blocks = jnp.zeros((2 * CHIPS, 1), I32)
    for p, s, lines in sources:
        i = 2 * p + s
        stacked = [jnp.where(row == i, line, old) for line, old in zip(lines, stacked)]
        blocks = jnp.where(row[:, 0:1] == i, 2 * (z ^ p) + (c ^ s), blocks)
    mine = 2 * z + c
    named = [stacked[k].astype(I32) == mine for k in range(2)]
    either = jnp.logical_or(named[0], named[1])
    before = lax.broadcasted_iota(I32, (toks, toks), 0) < lax.broadcasted_iota(
        I32, (toks, toks), 1
    )
    hits = either.astype(F32)
    rank = dot(hits.astype(BF16), before.astype(F32).astype(BF16)).astype(I32)
    count = jnp.sum(hits, axis=1, keepdims=True)
    earlier = jnp.zeros((2 * CHIPS, 1), F32)
    for p, s, _ in sources:
        i = 2 * p + s
        ahead = (2 * (z ^ p) + (c ^ s) < blocks).astype(F32)
        earlier = earlier + ahead * count[i : i + 1, :]
    keep = rank + earlier.astype(I32) < room_of(mine, cap, plan, extra_slots)
    weight = jnp.where(keep, 1.0, 0.0) * (
        named[0].astype(F32) * stacked[2] + named[1].astype(F32) * stacked[3]
    )
    for i in range(2 * CHIPS):
        hot = pick(rank, either, i, per)
        value = jnp.sum(hot * weight[i : i + 1, :], axis=1, keepdims=True)
        at = i % 4 * per
        (near_scale, far_scale)[i // 4][at : at + per, :] = jnp.broadcast_to(value, (per, 128))


def load_kernel(a, b, c, after, x, y, z, sems):
    copies = [
        pltpu.make_async_copy(src, dst, sems.at[i])
        for i, (src, dst) in enumerate(((a, x), (b, y), (c, z)))
    ]
    for copy in copies:
        copy.start()
    for copy in copies:
        copy.wait()


def combine(per, src, k, rows, info):
    slot = info[:, 2 * src + k : 2 * src + k + 1].astype(I32) - 1
    slots = lax.broadcasted_iota(I32, (info.shape[0], CHIPS * per), 1)
    return dot((slots == slot).astype(F32).astype(BF16), rows)


def back_kernel(per, with_dots, at0, feats, y0, y1, y2, y3, info_ref, *refs):
    if with_dots:
        own_g, par_g, kept, sent, kept_dots, sent_dots = refs
    else:
        kept, sent = refs
    info = info_ref[...]
    toks = info.shape[0]
    starts = [at0 if y.shape[1] > feats else 0 for y in (y0, y1, y2, y3)]
    lane = lax.broadcasted_iota(I32, (toks, 128), 1)
    for src, out in enumerate((kept, sent)):
        rows = jnp.concatenate(
            [
                y[src * per : (src + 1) * per, at : at + feats]
                for y, at in zip((y0, y1, y2, y3), starts)
            ],
            axis=0,
        )
        total = jnp.zeros((toks, feats), F32)
        dots = jnp.zeros((toks, 128), F32)
        for k in range(2):
            picked = combine(per, src, k, rows, info)
            at = 2 * src + k
            total = total + info[:, 4 + at : 5 + at] * picked
            if with_dots:
                grad = (own_g, par_g)[src][...].astype(F32)
                inner = jnp.sum(grad * picked, axis=1, keepdims=True) * info[:, 8 + at : 9 + at]
                dots = jnp.where(lane == k, inner, dots)
        out[...] = total.astype(out.dtype)
        if with_dots:
            (kept_dots, sent_dots)[src][...] = jnp.transpose(dots)[0:8, :]


def assemble(r, shards, at, feats, cat, scale):
    own, a, b, c, d = shards
    rows = own.shape[0]
    half = rows // 2
    lanes = slice(at, at + feats)
    factor = None if scale is None else scale[:, 0:1]
    for k, start, ref in ((0, 0, own), (1, 0, a), (2, 0, b), (3, 0, c), (3, half, d)):
        cols = pl.ds(pl.multiple_of((r ^ k) * feats, feats), feats)
        size = ref.shape[0]
        piece = ref[:, lanes]
        if factor is not None:
            piece = (piece.astype(F32) * factor[start : start + size, :]).astype(BF16)
        cat[start : start + size, cols] = piece


def split_out(part, outs, feats, low, high):
    send_a, keep_a, send_b, keep_b = outs
    half = send_a.shape[0]
    low, high = slice(low, low + feats), slice(high, high + feats)
    for k in (3, 1, 2, 0):
        piece = part(k).astype(BF16)
        top = ((keep_a, low), (send_a, low), (keep_a, high), (send_a, high))[k]
        bottom = ((keep_b, low), (keep_b, high), (send_b, low), (send_b, high))[k]
        top[0][:, top[1]] = piece[0:half, :]
        bottom[0][:, bottom[1]] = piece[half : 2 * half, :]


def forward(r, shards, wg, wu, wd, cat, hid, act, slope, outs, low, high):
    feats = shards[0].shape[1] // 2
    assemble(r, shards, 0, feats, cat, None)
    step = 256
    for j in range(0, hid.shape[1], step):
        cols = slice(j, j + step)
        gate = dot(cat[...], wg[:, cols])
        up = dot(cat[...], wu[:, cols])
        sig = jax.nn.sigmoid(gate)
        silu = gate * sig
        hid[:, cols] = (silu * up).astype(BF16)
        act[:, cols] = silu.astype(act.dtype)
        slope[:, cols] = (up * (sig + silu * (1.0 - sig))).astype(slope.dtype)

    def part(k):
        return dot(hid[...], wd[:, pl.ds(pl.multiple_of((r ^ k) * feats, feats), feats)])

    split_out(part, outs, feats, low, high)


def backward(r, shards, scale, wg, wu, wd, act, slope, cat, dgate, dup, outs, low, high):
    feats = shards[0].shape[1] // 2
    assemble(r, shards, feats, feats, cat, scale)
    step = 256
    for j in range(0, dgate.shape[1], step):
        cols = slice(j, j + step)
        dh = dot(cat[...], wd[cols, :], ((1,), (1,)))
        dgate[:, cols] = (dh * slope[:, cols].astype(F32)).astype(BF16)
        dup[:, cols] = (dh * act[:, cols].astype(F32)).astype(BF16)

    def part(k):
        line = pl.ds(pl.multiple_of((r ^ k) * feats, feats), feats)
        return dot(dgate[...], wg[line, :], ((1,), (1,))) + dot(dup[...], wu[line, :], ((1,), (1,)))

    split_out(part, outs, feats, low, high)


def near_kernel(ids, *refs):
    shards, (scale, wg, wu, wd), refs = refs[:5], refs[5:9], refs[9:]
    (xcat, hid, gcat, dgate, dup), outs, (act, slope) = refs[:5], refs[5:9], refs[9:]
    r, feats = ids[2], shards[0].shape[1] // 2
    forward(r, shards, wg, wu, wd, xcat, hid, act, slope, outs, 0, 2 * feats)
    backward(r, shards, scale, wg, wu, wd, act, slope, gcat, dgate, dup, outs, feats, 3 * feats)


def far_forward_kernel(ids, *refs):
    shards, (wg, wu, wd), (xcat, hid, act, slope), outs = refs[:5], refs[5:8], refs[8:12], refs[12:]
    feats = shards[0].shape[1] // 2
    forward(ids[2], shards, wg, wu, wd, xcat, hid, act, slope, outs, 0, feats)


def far_backward_kernel(ids, *refs):
    shards, (scale, wg, wu, wd, act, slope) = refs[:5], refs[5:11]
    (gcat, dgate, dup), outs = refs[11:14], refs[14:]
    feats = shards[0].shape[1] // 2
    backward(ids[2], shards, scale, wg, wu, wd, act, slope, gcat, dgate, dup, outs, 0, feats)


def weights_kernel(left_a, left_b, right_a, right_b, after, out, done):
    done[...] = jnp.zeros_like(done)
    size = out.shape[0]
    cols = pl.ds(pl.multiple_of(pl.program_id(0) * size, size), size)
    out[...] = dot(left_a[:, cols], right_a[...], ((0,), (0,))) + dot(
        left_b[:, cols], right_b[...], ((0,), (0,))
    )


def join_kernel(a, b, out):
    size = out.shape[0] // 2
    out[0:size, :] = a[0:size, :]
    out[size : 2 * size, :] = b[0:size, :]


def middle_kernel(ka, ra, kb, rb, sa, sb, kept):
    half, feats = sa.shape
    kept[0:half, :] = ka[:, 0:feats].astype(F32) + ra[:, 0:feats].astype(F32)
    kept[half : 2 * half, :] = kb[:, 0:feats].astype(F32) + rb[:, 0:feats].astype(F32)
    sa[...] = (ka[:, feats:].astype(F32) + ra[:, feats:].astype(F32)).astype(BF16)
    sb[...] = (kb[:, feats:].astype(F32) + rb[:, feats:].astype(F32)).astype(BF16)


def last_kernel(kept, ra, rb, *outs):
    half = ra.shape[0]
    size = outs[0].shape[0]
    for q, out in enumerate(outs):
        at = q * size
        other = ra[at : at + size, :] if at < half else rb[at - half : at - half + size, :]
        out[...] = (kept[at : at + size, :] + other.astype(F32)).astype(BF16)


def shift(x, axis, bit):
    n = lax.axis_size(axis)
    return lax.ppermute(x, axis, [(i, i ^ bit) for i in range(n)])


def sds(shape, dtype):
    return jax.ShapeDtypeStruct(shape, dtype)


def vm(shape, dtype):
    return pltpu.VMEM(shape, dtype)


def pin(*arrays):
    return [pltpu.with_memory_space_constraint(x, pltpu.VMEM) for x in arrays]


def grad_kernel(per, feats, y0, y1, y2, y3, info, dots, here, got, kept, sent, dots_out, mixed):
    back_kernel(per, False, feats, feats, y0, y1, y2, y3, info, kept, sent)
    mixed[...] = (here[...] + got[...].astype(F32)).astype(BF16)
    dots_out[...] = dots[...]


def kernel_call(body, name, outs, *args, plan_args=0, loose=0, flops=1, after=(), scratch=()):
    count = len(args)
    pinned = list(args[:plan_args])
    for x in args[plan_args : plan_args + loose]:
        pinned.append(pltpu.with_memory_space_constraint(x, pltpu.HBM))
    pinned += pin(*args[plan_args + loose :], *after)

    def run(*refs):
        body(*refs[:count], *refs[count + len(after) :])

    return pl.pallas_call(
        run,
        in_specs=[smem()] * plan_args + [vmem()] * (count - plan_args + len(after)),
        out_shape=outs,
        scratch_shapes=scratch,
        compiler_params=params(),
        cost_estimate=pl.CostEstimate(flops=flops, bytes_accessed=1 << 20, transcendentals=0),
        name=name,
    )(*pinned)


def relay_kernel(a, b, top, bottom):
    half = top.shape[0]
    top[...] = a[0:half, :]
    bottom[...] = b[half : 2 * half, :]


def gather_first(x):
    return x, shift(x, "rep", 1), shift(x, "rep", 2)


def gather_second(parts, after):
    x, a, b = parts
    half = vm((x.shape[0] // 2, x.shape[1]), BF16)
    top, bottom = kernel_call(relay_kernel, "relay", (half, half), a, b, after=after)
    return x, a, b, shift(top, "rep", 2), shift(bottom, "rep", 1)


def reduce_first(sa, ka, sb, kb):
    return ka, shift(sa, "rep", 1), kb, shift(sb, "rep", 2)


def reduce_second(parts, after=()):
    half, feats = parts[0].shape[0], parts[0].shape[1] // 2
    piece = vm((half, feats), BF16)
    ma, mb, kept = kernel_call(
        middle_kernel, "reduce_middle", (piece, piece, vm((2 * half, feats), F32)), *parts, after=after
    )
    return kept, shift(ma, "rep", 2), shift(mb, "rep", 1)


def reduce_last(parts, size, after=()):
    rows, feats = parts[0].shape
    outs = (vm((size, feats), BF16),) * (rows // size)
    return kernel_call(last_kernel, "reduce_last", outs, *parts, after=after)


def over_chips(chunks):
    return over_chips_from(0, chunks)


def over_chips_from(first, chunks):
    return [c if first + n == 0 else shift(c, "exp", 2 * (first + n)) for n, c in enumerate(chunks)]


def on_quad(tokens, routes, probs, capacity, plan, grad_out, w_gate, w_up, w_down):
    toks, feats = tokens.shape
    per = 4 * toks // capacity.shape[0]
    wg, wu, wd = w_gate[0], w_up[0], w_down[0]
    width, ff = wg.shape
    rows = 2 * per * CHIPS
    me = lax.axis_index("exp").astype(I32)
    ids = jnp.stack([me // 2, me % 2, lax.axis_index("rep").astype(I32)])
    own_m = (routes.T, probs.T)
    par_m = tuple(shift(x, "exp", 1) for x in own_m)
    par_x = shift(tokens, "exp", 1)
    par_g = shift(grad_out, "exp", 1)

    size = 2 * per
    both = 2 * feats
    stay = vm((size, both), BF16)
    go = vm((size + 16, both), BF16)
    sent = kernel_call(
        functools.partial(send_kernel, per),
        "send",
        (stay, go, go, go),
        ids, tokens, grad_out, *own_m, *par_m, par_x, par_g,
        plan_args=1,
        loose=2,
    )
    got = over_chips(sent)
    pair_rows = vm((2 * size, both), BF16)
    near = gather_first(kernel_call(join_kernel, "join_near", pair_rows, got[0], got[1]))
    loaded = vm((width, ff), BF16)
    wg, wu, wd = pl.pallas_call(
        load_kernel,
        in_specs=[pl.BlockSpec(memory_space=pltpu.HBM)] * 3 + [vmem()],
        out_shape=(loaded, loaded, vm((ff, width), BF16)),
        scratch_shapes=[pltpu.SemaphoreType.DMA((3,))],
        compiler_params=params(),
        cost_estimate=pl.CostEstimate(flops=2*10**10, bytes_accessed=24 << 20, transcendentals=0),
        name="load_weights",
    )(*[pltpu.with_memory_space_constraint(w, pltpu.HBM) for w in (wg, wu, wd)], *pin(near[0]))
    far = gather_first(
        kernel_call(join_kernel, "join_far", pair_rows, got[2], got[3], after=(wg,))
    )
    info, near_scale, far_scale = kernel_call(
        functools.partial(place_kernel, per, 2 * toks),
        "place",
        (vm((toks, 128), F32), vm((2 * size, 128), F32), vm((2 * size, 128), F32)),
        ids, capacity, plan, *own_m, *par_m, *got[1:],
        plan_args=3,
    )
    near = gather_second(near, (far[0],))

    inner = vm((2 * size, ff), BF16)
    wide = vm((2 * size, width), BF16)
    work = 2 * (2 * size) * width * ff
    near_x, near_hid, near_g, near_dgate, near_dup, *near_parts = kernel_call(
        near_kernel,
        "near",
        (wide, inner, wide, inner, inner) + (vm((size, 2 * both), BF16),) * 4,
        ids, *near, near_scale, wg, wu, wd,
        plan_args=1,
        flops=6 * work,
        scratch=[pltpu.VMEM((2 * size, ff), F32)] * 2,
    )
    far = gather_second(far, (near_hid,))
    near_first = reduce_first(*near_parts)
    part = vm((size, both), BF16)
    far_x, far_hid, act, slope, *out_parts = kernel_call(
        far_forward_kernel,
        "far_forward",
        (wide, inner, inner, inner) + (part,) * 4,
        ids, *far, wg, wu, wd,
        plan_args=1,
        flops=3 * work,
    )
    out_first = reduce_first(*out_parts)
    far_g, far_dgate, far_dup, *dx_parts = kernel_call(
        far_backward_kernel,
        "far_backward",
        (wide, inner, inner) + (part,) * 4,
        ids, *far, far_scale, wg, wu, wd, act, slope,
        plan_args=1,
        flops=3 * work,
        after=(out_parts[0], near_first[1], near_first[3]),
    )
    dx_first = reduce_first(*dx_parts)

    def weight_grad(name, left, right, n, m, after):
        steps = 4
        return pl.pallas_call(
            weights_kernel,
            grid=(steps,),
            in_specs=[vmem()] * 5,
            out_specs=[pl.BlockSpec((n // steps, m), lambda i: (i, 0)), vmem()],
            out_shape=(sds((n, m), F32), vm((8, 128), F32)),
            compiler_params=params(),
            cost_estimate=pl.CostEstimate(flops=2*10**10, bytes_accessed=1, transcendentals=0),
            name=name,
        )(*pin(*left, *right, after))

    out_sums = reduce_second(out_first, (far_dgate,))
    near_sums = reduce_second(near_first, (out_sums[0],))
    grad_down, done_d = weight_grad(
        "grad_down", (near_hid, far_hid), (near_g, far_g), ff, width, out_sums[0]
    )
    dx_sums = reduce_second(dx_first, (done_d,))
    out_rows = reduce_last(out_sums, size, (dx_sums[0],))
    back_out = over_chips_from(2, out_rows)
    grad_gate, done_g = weight_grad(
        "grad_gate", (near_x, far_x), (near_dgate, far_dgate), width, ff, out_rows[0]
    )
    dx_rows = reduce_last(dx_sums, size, (done_g,))
    back_dx = over_chips_from(2, dx_rows)
    near_rows = reduce_last(near_sums, size, dx_rows[:1])
    back_near = over_chips_from(0, near_rows)
    grad_up, done_u = weight_grad(
        "grad_up", (near_x, far_x), (near_dup, far_dup), width, ff, near_rows[0]
    )

    whole, narrow, few = vm((toks, feats), F32), vm((toks, feats), BF16), vm((8, toks), F32)
    kept, sent, kept_dots, sent_dots = kernel_call(
        functools.partial(back_kernel, per, True, 0, feats),
        "combine_out",
        (whole, narrow, few, few),
        *back_near, *back_out, info, grad_out, par_g,
        after=(done_u,),
    )
    dots = kept_dots + shift(sent_dots, "exp", 1)
    kept, sent, dots, mixed = kernel_call(
        functools.partial(grad_kernel, per, feats),
        "combine_grad",
        (whole, narrow, few, sds((toks, feats), BF16)),
        *back_near, *back_dx, info, dots, kept, shift(sent, "exp", 1),
    )
    first = dots[0:2]
    second, third, fourth = (shift(first, "rep", k) for k in (1, 2, 3))
    grad_probs = ((first + second) + (third + fourth)).T
    grad_tokens = (kept + shift(sent, "exp", 1).astype(F32)).astype(BF16)
    return (mixed, grad_tokens, grad_probs, grad_gate[None], grad_up[None], grad_down[None])


def solution(mesh):
    sizes = dict(mesh.shape)
    fast = sizes["rep"] == 4 and sizes["exp"] == 8
    return jax.shard_map(
        on_quad if fast else on_device,
        mesh=mesh,
        in_specs=(
            P("exp", "rep"),
            P("exp", None),
            P("exp", None),
            P(),
            P(),
            P("exp", "rep"),
            P("exp", None, "rep"),
            P("exp", None, "rep"),
            P("exp", "rep", None),
        ),
        out_specs=(
            P("exp", "rep"),
            P("exp", "rep"),
            P("exp", None),
            P("exp", None, "rep"),
            P("exp", None, "rep"),
            P("exp", "rep", None),
        ),
        check_vma=False,
    )
```

```python
import functools

import jax
import jax.numpy as jnp
from jax import lax
from jax.experimental import pallas as pl
from jax.experimental.pallas import tpu as pltpu
from jax.sharding import PartitionSpec as P

HOT = 4


def carried_in(value, axis, combine, identity):
    peers, mine = (lax.axis_size(axis), lax.axis_index(axis))
    everything = lax.all_gather(value, axis)
    start = jnp.broadcast_to(jnp.asarray(identity, value.dtype), value.shape)

    def step(k, before):
        reached = k < mine
        new = combine(before, everything[k])
        return jnp.where(reached, new, before)

    return lax.fori_loop(0, peers, step, start)


def fill_rows(shard, flat, rank, token_of, scale, experts, per_slot):
    picked = shard[token_of]
    if scale is not None:
        picked = (picked.astype(jnp.float32) * scale[:, None]).astype(jnp.bfloat16)
    empty = jnp.zeros((experts, per_slot, shard.shape[1]), jnp.bfloat16)
    return empty.at[flat, rank].set(picked)


def dispatch(shard, flat, rank, token_of, scale, experts, per_slot):
    buffer = fill_rows(shard, flat, rank, token_of, scale, experts, per_slot)
    received = lax.all_to_all(buffer, "exp", split_axis=0, concat_axis=0, tiled=True)
    narrow = received.reshape(-1, received.shape[2])
    return lax.all_gather(narrow, "rep", axis=1, tiled=True)


def return_rows(rows, flat, rank, experts, per_slot):
    back = lax.all_to_all(
        rows.reshape(experts, per_slot, rows.shape[1]),
        "exp",
        split_axis=0,
        concat_axis=0,
        tiled=True,
    )
    return back[flat, rank].astype(jnp.float32)


def on_device(tokens, routes, probs, capacity, plan, grad_out, w_gate, w_up, w_down):
    tok_rows = tokens.shape[0]
    experts = capacity.shape[0]
    per_slot = 4 * tok_rows // experts
    feat_cols = tokens.shape[1]
    flat = routes.reshape(-1)
    expert_ids = jnp.arange(experts, dtype=jnp.int32)
    onehot = (flat[:, None] == expert_ids[None, :]).astype(jnp.int32)
    rank = jnp.sum((jnp.cumsum(onehot, axis=0) - onehot) * onehot, axis=1)
    counts = jnp.sum(onehot, axis=0)
    earlier = carried_in(
        counts, "exp", lambda first, second: first + second, jnp.zeros_like(counts)
    )
    position = rank + jnp.sum(onehot * earlier[None, :], axis=1)
    hot_flag = jnp.any(plan[:HOT][:, None] == expert_ids[None, :], axis=0).astype(jnp.int32)
    limit = capacity + 2 * tok_rows * hot_flag
    keep = (position < jnp.sum(onehot * limit[None, :], axis=1)).astype(jnp.float32)
    weight = probs.reshape(-1) * keep
    token_of = jnp.arange(2 * tok_rows, dtype=jnp.int32) // 2
    wg = w_gate[0]
    wu = w_up[0]
    wd = w_down[0]
    xs = dispatch(tokens, flat, rank, token_of, None, experts, per_slot)
    gate = jnp.dot(xs, wg, preferred_element_type=jnp.float32)
    up = jnp.dot(xs, wu, preferred_element_type=jnp.float32)
    sig = jax.nn.sigmoid(gate)
    silu = gate * sig
    hidden = (silu * up).astype(jnp.bfloat16)
    partial_value = jnp.dot(hidden, wd, preferred_element_type=jnp.float32)
    out_rows = lax.psum_scatter(
        partial_value.astype(jnp.bfloat16), "rep", scatter_dimension=1, tiled=True
    )
    picked = return_rows(out_rows, flat, rank, experts, per_slot)
    mixed = jnp.sum((weight[:, None] * picked).reshape(tok_rows, 2, feat_cols), axis=1).astype(
        jnp.bfloat16
    )
    dots = jnp.sum(grad_out[token_of].astype(jnp.float32) * picked, axis=1)
    dots = lax.psum(dots, "rep")
    grad_probs = (keep * dots).reshape(tok_rows, 2)
    dout = dispatch(grad_out, flat, rank, token_of, weight, experts, per_slot)
    dh = lax.dot_general(dout, wd, (((1,), (1,)), ((), ())), preferred_element_type=jnp.float32)
    dgate = (dh * up * sig * (1.0 + gate * (1.0 - sig))).astype(jnp.bfloat16)
    dup = (dh * silu).astype(jnp.bfloat16)
    grad_down = lax.dot_general(
        hidden, dout, (((0,), (0,)), ((), ())), preferred_element_type=jnp.float32
    )
    grad_gate = lax.dot_general(
        xs, dgate, (((0,), (0,)), ((), ())), preferred_element_type=jnp.float32
    )
    grad_up = lax.dot_general(xs, dup, (((0,), (0,)), ((), ())), preferred_element_type=jnp.float32)
    dpartial = lax.dot_general(
        dgate, wg, (((1,), (1,)), ((), ())), preferred_element_type=jnp.float32
    )
    dpartial = dpartial + lax.dot_general(
        dup, wu, (((1,), (1,)), ((), ())), preferred_element_type=jnp.float32
    )
    dx_rows = lax.psum_scatter(
        dpartial.astype(jnp.bfloat16), "rep", scatter_dimension=1, tiled=True
    )
    back = return_rows(dx_rows, flat, rank, experts, per_slot)
    grad_tokens = jnp.sum((weight[:, None] * back).reshape(tok_rows, 2, feat_cols), axis=1).astype(
        jnp.bfloat16
    )
    return (mixed, grad_tokens, grad_probs, grad_gate[None], grad_up[None], grad_down[None])


F32 = jnp.float32
BF16 = jnp.bfloat16
I32 = jnp.int32
CHIPS = 4
VMEM_BYTES = 14 * 1024 * 1024


def dot(a, b, dims=((1,), (0,))):
    return lax.dot_general(a, b, (dims, ((), ())), preferred_element_type=F32)


def params(**kw):
    return pltpu.CompilerParams(vmem_limit_bytes=VMEM_BYTES, **kw)


def vmem():
    return pl.BlockSpec(memory_space=pltpu.VMEM)


def smem():
    return pl.BlockSpec(memory_space=pltpu.SMEM)


def table_of(routes, probs):
    return jnp.concatenate([routes[...].astype(F32), probs[...]], axis=0)


def place_rows(ids, own, par, per):
    z, c = ids[0], ids[1]
    toks = own.shape[1]
    row = lax.broadcasted_iota(I32, (2 * CHIPS, toks), 0)
    expert = 2 * (z ^ (row % CHIPS)) + c
    first = row < CHIPS
    named = [
        jnp.where(first, own[k : k + 1, :], par[k : k + 1, :]).astype(I32) == expert
        for k in range(2)
    ]
    either = jnp.logical_or(named[0], named[1])
    before = lax.broadcasted_iota(I32, (toks, toks), 0) < lax.broadcasted_iota(
        I32, (toks, toks), 1
    )
    rank = dot(either.astype(F32).astype(BF16), before.astype(F32).astype(BF16)).astype(I32)
    return row, expert, named, either, rank


def pick(rank, either, i, per):
    at = jnp.where(either[i : i + 1, :], rank[i : i + 1, :], -1)
    slots = lax.broadcasted_iota(I32, (per, at.shape[1]), 0)
    return (slots == at).astype(F32)


def thirds(line):
    high = line.astype(BF16).astype(F32)
    middle = (line - high).astype(BF16).astype(F32)
    return high, middle, line - high - middle


def send_kernel(per, ids, own_x, own_g, own_r, own_p, par_r, par_p, par_x, par_g, c0, c1, c2, c3):
    own, par = table_of(own_r, own_p), table_of(par_r, par_p)
    toks = own.shape[1]
    feats = own_x.shape[1]
    _, _, _, either, rank = place_rows(ids, own, par, per)
    tail = lax.broadcasted_iota(I32, (16, toks), 0)
    lines = [own[0:1, :], own[1:2, :], par[0:1, :], par[1:2, :]]
    for table in (own, par):
        for k in range(2):
            lines += thirds(table[2 + k : 3 + k, :])
    extra = jnp.zeros((16, toks), F32)
    for i, line in enumerate(lines):
        extra = jnp.where(tail == i, line, extra)
    for q, out in enumerate((c0, c1, c2, c3)):
        for src in range(2):
            hot = pick(rank, either, CHIPS * src + q, per).astype(BF16)
            place = slice(src * per, (src + 1) * per)
            out[place, 0:feats] = dot(hot, (own_x, par_x)[src][...]).astype(BF16)
            out[place, feats : 2 * feats] = dot(hot, (own_g, par_g)[src][...]).astype(BF16)
        if q:
            out[2 * per : 2 * per + 16, 0:toks] = extra.astype(BF16)
            out[2 * per : 2 * per + 16, toks : 2 * toks] = jnp.zeros((16, toks), BF16)


def room_of(e, cap, plan, extra_slots):
    room = cap[e]
    for h in range(HOT):
        room = room + jnp.where(plan[h] == e, extra_slots, 0)
    return room


def place_kernel(per, extra_slots, ids, cap, plan, own_r, own_p, par_r, par_p, e1, e2, e3, info, near_scale, far_scale):
    own, par = table_of(own_r, own_p), table_of(par_r, par_p)
    toks = own.shape[1]
    z, c = ids[0], ids[1]
    row, expert, named, either, rank = place_rows(ids, own, par, per)
    q_col = row[:, 0:1] % CHIPS
    first = row < CHIPS
    first_col = first[:, 0:1]

    sources = []
    for s, table in enumerate((own, par)):
        sources.append((0, s, [table[k : k + 1, :] for k in range(4)]))
    for p, ref in ((1, e1), (2, e2), (3, e3)):
        table = ref[2 * per : 2 * per + 16, 0:toks].astype(F32)
        for s in range(2):
            lines = [table[2 * s + k : 2 * s + k + 1, :] for k in range(2)]
            for k in range(2):
                at = 4 + 3 * (2 * s + k)
                lines.append(
                    table[at : at + 1, :] + table[at + 1 : at + 2, :] + table[at + 2 : at + 3, :]
                )
            sources.append((p, s, lines))

    limit = jnp.zeros((2 * CHIPS, 1), I32)
    for q in range(CHIPS):
        limit = jnp.where(q_col == q, room_of(2 * (z ^ q) + c, cap, plan, extra_slots), limit)
    earlier = jnp.zeros((2 * CHIPS, 1), F32)
    for p, s, lines in sources:
        hits = jnp.logical_or(lines[0].astype(I32) == expert, lines[1].astype(I32) == expert)
        count = jnp.sum(hits.astype(F32), axis=1, keepdims=True)
        block = 2 * (z ^ p) + (c ^ s)
        ahead = jnp.where(
            first_col,
            (block < 2 * z + c).astype(F32),
            (block < 2 * z + (c ^ 1)).astype(F32),
        )
        earlier = earlier + count * ahead
    keep = jnp.where(rank + earlier.astype(I32) < limit, 1.0, 0.0)
    kinds = []
    for k in range(2):
        prob = jnp.where(first, own[2 + k : 3 + k, :], par[2 + k : 3 + k, :])
        mine = named[k].astype(F32)
        slot = (row % CHIPS * per + rank + 1).astype(F32)
        kinds.append((mine * slot, mine * keep * prob, mine * keep))
    at = lax.broadcasted_iota(I32, (128, toks), 0)
    table = jnp.zeros((128, toks), F32)
    for kind in range(3):
        for src in range(2):
            half = first if src == 0 else jnp.logical_not(first)
            for k in range(2):
                line = jnp.sum(jnp.where(half, kinds[k][kind], 0.0), axis=0, keepdims=True)
                table = jnp.where(at == 4 * kind + 2 * src + k, line, table)
    info[...] = jnp.transpose(table)

    stacked = [jnp.zeros((2 * CHIPS, toks), F32) for _ in range(4)]
    blocks = jnp.zeros((2 * CHIPS, 1), I32)
    for p, s, lines in sources:
        i = 2 * p + s
        stacked = [jnp.where(row == i, line, old) for line, old in zip(lines, stacked)]
        blocks = jnp.where(row[:, 0:1] == i, 2 * (z ^ p) + (c ^ s), blocks)
    mine = 2 * z + c
    named = [stacked[k].astype(I32) == mine for k in range(2)]
    either = jnp.logical_or(named[0], named[1])
    before = lax.broadcasted_iota(I32, (toks, toks), 0) < lax.broadcasted_iota(
        I32, (toks, toks), 1
    )
    hits = either.astype(F32)
    rank = dot(hits.astype(BF16), before.astype(F32).astype(BF16)).astype(I32)
    count = jnp.sum(hits, axis=1, keepdims=True)
    earlier = jnp.zeros((2 * CHIPS, 1), F32)
    for p, s, _ in sources:
        i = 2 * p + s
        ahead = (2 * (z ^ p) + (c ^ s) < blocks).astype(F32)
        earlier = earlier + ahead * count[i : i + 1, :]
    keep = rank + earlier.astype(I32) < room_of(mine, cap, plan, extra_slots)
    weight = jnp.where(keep, 1.0, 0.0) * (
        named[0].astype(F32) * stacked[2] + named[1].astype(F32) * stacked[3]
    )
    for i in range(2 * CHIPS):
        hot = pick(rank, either, i, per)
        value = jnp.sum(hot * weight[i : i + 1, :], axis=1, keepdims=True)
        at = i % 4 * per
        (near_scale, far_scale)[i // 4][at : at + per, :] = jnp.broadcast_to(value, (per, 128))


def load_kernel(a, b, c, after, x, y, z, sems):
    copies = [
        pltpu.make_async_copy(src, dst, sems.at[i])
        for i, (src, dst) in enumerate(((a, x), (b, y), (c, z)))
    ]
    for copy in copies:
        copy.start()
    for copy in copies:
        copy.wait()


def combine(per, src, k, rows, info):
    slot = info[:, 2 * src + k : 2 * src + k + 1].astype(I32) - 1
    slots = lax.broadcasted_iota(I32, (info.shape[0], CHIPS * per), 1)
    return dot((slots == slot).astype(F32).astype(BF16), rows)


def back_kernel(per, with_dots, at0, feats, y0, y1, y2, y3, info_ref, *refs):
    if with_dots:
        own_g, par_g, kept, sent, kept_dots, sent_dots = refs
    else:
        kept, sent = refs
    info = info_ref[...]
    toks = info.shape[0]
    starts = [at0 if y.shape[1] > feats else 0 for y in (y0, y1, y2, y3)]
    lane = lax.broadcasted_iota(I32, (toks, 128), 1)
    for src, out in enumerate((kept, sent)):
        rows = jnp.concatenate(
            [
                y[src * per : (src + 1) * per, at : at + feats]
                for y, at in zip((y0, y1, y2, y3), starts)
            ],
            axis=0,
        )
        total = jnp.zeros((toks, feats), F32)
        dots = jnp.zeros((toks, 128), F32)
        for k in range(2):
            picked = combine(per, src, k, rows, info)
            at = 2 * src + k
            total = total + info[:, 4 + at : 5 + at] * picked
            if with_dots:
                grad = (own_g, par_g)[src][...].astype(F32)
                inner = jnp.sum(grad * picked, axis=1, keepdims=True) * info[:, 8 + at : 9 + at]
                dots = jnp.where(lane == k, inner, dots)
        out[...] = total.astype(out.dtype)
        if with_dots:
            (kept_dots, sent_dots)[src][...] = jnp.transpose(dots)[0:8, :]


def assemble(r, shards, at, feats, cat, scale):
    own, a, b, c, d = shards
    rows = own.shape[0]
    half = rows // 2
    lanes = slice(at, at + feats)
    factor = None if scale is None else scale[:, 0:1]
    for k, start, ref in ((0, 0, own), (1, 0, a), (2, 0, b), (3, 0, c), (3, half, d)):
        cols = pl.ds(pl.multiple_of((r ^ k) * feats, feats), feats)
        size = ref.shape[0]
        piece = ref[:, lanes]
        if factor is not None:
            piece = (piece.astype(F32) * factor[start : start + size, :]).astype(BF16)
        cat[start : start + size, cols] = piece


def split_out(part, outs, feats, low, high):
    send_a, keep_a, send_b, keep_b = outs
    half = send_a.shape[0]
    low, high = slice(low, low + feats), slice(high, high + feats)
    for k in (3, 1, 2, 0):
        piece = part(k).astype(BF16)
        top = ((keep_a, low), (send_a, low), (keep_a, high), (send_a, high))[k]
        bottom = ((keep_b, low), (keep_b, high), (send_b, low), (send_b, high))[k]
        top[0][:, top[1]] = piece[0:half, :]
        bottom[0][:, bottom[1]] = piece[half : 2 * half, :]


def forward(r, shards, wg, wu, wd, cat, hid, act, slope, outs, low, high):
    feats = shards[0].shape[1] // 2
    assemble(r, shards, 0, feats, cat, None)
    step = 256
    for j in range(0, hid.shape[1], step):
        cols = slice(j, j + step)
        gate = dot(cat[...], wg[:, cols])
        up = dot(cat[...], wu[:, cols])
        sig = jax.nn.sigmoid(gate)
        silu = gate * sig
        hid[:, cols] = (silu * up).astype(BF16)
        act[:, cols] = silu.astype(act.dtype)
        slope[:, cols] = (up * (sig + silu * (1.0 - sig))).astype(slope.dtype)

    def part(k):
        return dot(hid[...], wd[:, pl.ds(pl.multiple_of((r ^ k) * feats, feats), feats)])

    split_out(part, outs, feats, low, high)


def backward(r, shards, scale, wg, wu, wd, act, slope, cat, dgate, dup, outs, low, high):
    feats = shards[0].shape[1] // 2
    assemble(r, shards, feats, feats, cat, scale)
    step = 256
    for j in range(0, dgate.shape[1], step):
        cols = slice(j, j + step)
        dh = dot(cat[...], wd[cols, :], ((1,), (1,)))
        dgate[:, cols] = (dh * slope[:, cols].astype(F32)).astype(BF16)
        dup[:, cols] = (dh * act[:, cols].astype(F32)).astype(BF16)

    def part(k):
        line = pl.ds(pl.multiple_of((r ^ k) * feats, feats), feats)
        return dot(dgate[...], wg[line, :], ((1,), (1,))) + dot(dup[...], wu[line, :], ((1,), (1,)))

    split_out(part, outs, feats, low, high)


def near_kernel(ids, *refs):
    shards, (scale, wg, wu, wd), refs = refs[:5], refs[5:9], refs[9:]
    (xcat, hid, gcat, dgate, dup), outs, (act, slope) = refs[:5], refs[5:9], refs[9:]
    r, feats = ids[2], shards[0].shape[1] // 2
    forward(r, shards, wg, wu, wd, xcat, hid, act, slope, outs, 0, 2 * feats)
    backward(r, shards, scale, wg, wu, wd, act, slope, gcat, dgate, dup, outs, feats, 3 * feats)


def far_forward_kernel(ids, *refs):
    shards, (wg, wu, wd), (xcat, hid, act, slope), outs = refs[:5], refs[5:8], refs[8:12], refs[12:]
    feats = shards[0].shape[1] // 2
    forward(ids[2], shards, wg, wu, wd, xcat, hid, act, slope, outs, 0, feats)


def far_backward_kernel(ids, *refs):
    shards, (scale, wg, wu, wd, act, slope) = refs[:5], refs[5:11]
    (gcat, dgate, dup), outs = refs[11:14], refs[14:]
    feats = shards[0].shape[1] // 2
    backward(ids[2], shards, scale, wg, wu, wd, act, slope, gcat, dgate, dup, outs, 0, feats)


def weights_kernel(left_a, left_b, right_a, right_b, after, out, done):
    done[...] = jnp.zeros_like(done)
    size = out.shape[0]
    cols = pl.ds(pl.multiple_of(pl.program_id(0) * size, size), size)
    out[...] = dot(left_a[:, cols], right_a[...], ((0,), (0,))) + dot(
        left_b[:, cols], right_b[...], ((0,), (0,))
    )


def join_kernel(a, b, out):
    size = out.shape[0] // 2
    out[0:size, :] = a[0:size, :]
    out[size : 2 * size, :] = b[0:size, :]


def middle_kernel(ka, ra, kb, rb, sa, sb, kept):
    half, feats = sa.shape
    kept[0:half, :] = ka[:, 0:feats].astype(F32) + ra[:, 0:feats].astype(F32)
    kept[half : 2 * half, :] = kb[:, 0:feats].astype(F32) + rb[:, 0:feats].astype(F32)
    sa[...] = (ka[:, feats:].astype(F32) + ra[:, feats:].astype(F32)).astype(BF16)
    sb[...] = (kb[:, feats:].astype(F32) + rb[:, feats:].astype(F32)).astype(BF16)


def last_kernel(kept, ra, rb, *outs):
    half = ra.shape[0]
    size = outs[0].shape[0]
    for q, out in enumerate(outs):
        at = q * size
        other = ra[at : at + size, :] if at < half else rb[at - half : at - half + size, :]
        out[...] = (kept[at : at + size, :] + other.astype(F32)).astype(BF16)


def shift(x, axis, bit):
    n = lax.axis_size(axis)
    return lax.ppermute(x, axis, [(i, i ^ bit) for i in range(n)])


def sds(shape, dtype):
    return jax.ShapeDtypeStruct(shape, dtype)


def vm(shape, dtype):
    return pltpu.VMEM(shape, dtype)


def pin(*arrays):
    return [pltpu.with_memory_space_constraint(x, pltpu.VMEM) for x in arrays]


def grad_kernel(per, feats, y0, y1, y2, y3, info, dots, here, got, kept, sent, dots_out, mixed):
    back_kernel(per, False, feats, feats, y0, y1, y2, y3, info, kept, sent)
    mixed[...] = (here[...] + got[...].astype(F32)).astype(BF16)
    dots_out[...] = dots[...]


def kernel_call(body, name, outs, *args, plan_args=0, loose=0, flops=1, after=(), scratch=()):
    count = len(args)
    pinned = list(args[:plan_args])
    for x in args[plan_args : plan_args + loose]:
        pinned.append(pltpu.with_memory_space_constraint(x, pltpu.HBM))
    pinned += pin(*args[plan_args + loose :], *after)

    def run(*refs):
        body(*refs[:count], *refs[count + len(after) :])

    return pl.pallas_call(
        run,
        in_specs=[smem()] * plan_args + [vmem()] * (count - plan_args + len(after)),
        out_shape=outs,
        scratch_shapes=scratch,
        compiler_params=params(),
        cost_estimate=pl.CostEstimate(flops=flops, bytes_accessed=1 << 20, transcendentals=0),
        name=name,
    )(*pinned)


def relay_kernel(a, b, top, bottom):
    half = top.shape[0]
    top[...] = a[0:half, :]
    bottom[...] = b[half : 2 * half, :]


def gather_first(x):
    return x, shift(x, "rep", 1), shift(x, "rep", 2)


def gather_second(parts, after):
    x, a, b = parts
    half = vm((x.shape[0] // 2, x.shape[1]), BF16)
    top, bottom = kernel_call(relay_kernel, "relay", (half, half), a, b, after=after)
    return x, a, b, shift(top, "rep", 2), shift(bottom, "rep", 1)


def reduce_first(sa, ka, sb, kb):
    return ka, shift(sa, "rep", 1), kb, shift(sb, "rep", 2)


def reduce_second(parts, after=()):
    half, feats = parts[0].shape[0], parts[0].shape[1] // 2
    piece = vm((half, feats), BF16)
    ma, mb, kept = kernel_call(
        middle_kernel, "reduce_middle", (piece, piece, vm((2 * half, feats), F32)), *parts, after=after
    )
    return kept, shift(ma, "rep", 2), shift(mb, "rep", 1)


def reduce_last(parts, size, after=()):
    rows, feats = parts[0].shape
    outs = (vm((size, feats), BF16),) * (rows // size)
    return kernel_call(last_kernel, "reduce_last", outs, *parts, after=after)


def over_chips(chunks):
    return over_chips_from(0, chunks)


def over_chips_from(first, chunks):
    return [c if first + n == 0 else shift(c, "exp", 2 * (first + n)) for n, c in enumerate(chunks)]


def on_quad(tokens, routes, probs, capacity, plan, grad_out, w_gate, w_up, w_down):
    toks, feats = tokens.shape
    per = 4 * toks // capacity.shape[0]
    wg, wu, wd = w_gate[0], w_up[0], w_down[0]
    width, ff = wg.shape
    rows = 2 * per * CHIPS
    me = lax.axis_index("exp").astype(I32)
    ids = jnp.stack([me // 2, me % 2, lax.axis_index("rep").astype(I32)])
    own_m = (routes.T, probs.T)
    par_m = tuple(shift(x, "exp", 1) for x in own_m)
    par_x = shift(tokens, "exp", 1)
    par_g = shift(grad_out, "exp", 1)

    size = 2 * per
    both = 2 * feats
    stay = vm((size, both), BF16)
    go = vm((size + 16, both), BF16)
    sent = kernel_call(
        functools.partial(send_kernel, per),
        "send",
        (stay, go, go, go),
        ids, tokens, grad_out, *own_m, *par_m, par_x, par_g,
        plan_args=1,
        loose=2,
    )
    got = over_chips(sent)
    pair_rows = vm((2 * size, both), BF16)
    near = gather_first(kernel_call(join_kernel, "join_near", pair_rows, got[0], got[1]))
    loaded = vm((width, ff), BF16)
    wg, wu, wd = pl.pallas_call(
        load_kernel,
        in_specs=[pl.BlockSpec(memory_space=pltpu.HBM)] * 3 + [vmem()],
        out_shape=(loaded, loaded, vm((ff, width), BF16)),
        scratch_shapes=[pltpu.SemaphoreType.DMA((3,))],
        compiler_params=params(),
        cost_estimate=pl.CostEstimate(flops=2*10**10, bytes_accessed=24 << 20, transcendentals=0),
        name="load_weights",
    )(*[pltpu.with_memory_space_constraint(w, pltpu.HBM) for w in (wg, wu, wd)], *pin(near[0]))
    far = gather_first(
        kernel_call(join_kernel, "join_far", pair_rows, got[2], got[3], after=(wg,))
    )
    info, near_scale, far_scale = kernel_call(
        functools.partial(place_kernel, per, 2 * toks),
        "place",
        (vm((toks, 128), F32), vm((2 * size, 128), F32), vm((2 * size, 128), F32)),
        ids, capacity, plan, *own_m, *par_m, *got[1:],
        plan_args=3,
    )
    near = gather_second(near, (far[0],))

    inner = vm((2 * size, ff), BF16)
    wide = vm((2 * size, width), BF16)
    work = 2 * (2 * size) * width * ff
    near_x, near_hid, near_g, near_dgate, near_dup, *near_parts = kernel_call(
        near_kernel,
        "near",
        (wide, inner, wide, inner, inner) + (vm((size, 2 * both), BF16),) * 4,
        ids, *near, near_scale, wg, wu, wd,
        plan_args=1,
        flops=6 * work,
        scratch=[pltpu.VMEM((2 * size, ff), F32)] * 2,
    )
    far = gather_second(far, (near_hid,))
    near_first = reduce_first(*near_parts)
    part = vm((size, both), BF16)
    far_x, far_hid, act, slope, *out_parts = kernel_call(
        far_forward_kernel,
        "far_forward",
        (wide, inner, inner, inner) + (part,) * 4,
        ids, *far, wg, wu, wd,
        plan_args=1,
        flops=3 * work,
    )
    out_first = reduce_first(*out_parts)
    far_g, far_dgate, far_dup, *dx_parts = kernel_call(
        far_backward_kernel,
        "far_backward",
        (wide, inner, inner) + (part,) * 4,
        ids, *far, far_scale, wg, wu, wd, act, slope,
        plan_args=1,
        flops=3 * work,
        after=(out_parts[0], near_first[1], near_first[3]),
    )
    dx_first = reduce_first(*dx_parts)

    def weight_grad(name, left, right, n, m, after):
        steps = 4
        return pl.pallas_call(
            weights_kernel,
            grid=(steps,),
            in_specs=[vmem()] * 5,
            out_specs=[pl.BlockSpec((n // steps, m), lambda i: (i, 0)), vmem()],
            out_shape=(sds((n, m), F32), vm((8, 128), F32)),
            compiler_params=params(),
            cost_estimate=pl.CostEstimate(flops=2*10**10, bytes_accessed=1, transcendentals=0),
            name=name,
        )(*pin(*left, *right, after))

    out_sums = reduce_second(out_first, (far_dgate,))
    near_sums = reduce_second(near_first, (out_sums[0],))
    grad_down, done_d = weight_grad(
        "grad_down", (near_hid, far_hid), (near_g, far_g), ff, width, out_sums[0]
    )
    dx_sums = reduce_second(dx_first, (done_d,))
    out_rows = reduce_last(out_sums, size, (dx_sums[0],))
    back_out = over_chips_from(2, out_rows)
    dx_rows = reduce_last(dx_sums, size, out_rows[:1])
    back_dx = over_chips_from(2, dx_rows)
    near_rows = reduce_last(near_sums, size, dx_rows[:1])
    back_near = over_chips_from(0, near_rows)
    grad_gate, done_g = weight_grad(
        "grad_gate", (near_x, far_x), (near_dgate, far_dgate), width, ff, near_rows[0]
    )
    grad_up, done_u = weight_grad(
        "grad_up", (near_x, far_x), (near_dup, far_dup), width, ff, done_g
    )

    whole, narrow, few = vm((toks, feats), F32), vm((toks, feats), BF16), vm((8, toks), F32)
    kept, sent, kept_dots, sent_dots = kernel_call(
        functools.partial(back_kernel, per, True, 0, feats),
        "combine_out",
        (whole, narrow, few, few),
        *back_near, *back_out, info, grad_out, par_g,
        after=(done_u,),
    )
    dots = kept_dots + shift(sent_dots, "exp", 1)
    kept, sent, dots, mixed = kernel_call(
        functools.partial(grad_kernel, per, feats),
        "combine_grad",
        (whole, narrow, few, sds((toks, feats), BF16)),
        *back_near, *back_dx, info, dots, kept, shift(sent, "exp", 1),
    )
    first = dots[0:2]
    second, third, fourth = (shift(first, "rep", k) for k in (1, 2, 3))
    grad_probs = ((first + second) + (third + fourth)).T
    grad_tokens = (kept + shift(sent, "exp", 1).astype(F32)).astype(BF16)
    return (mixed, grad_tokens, grad_probs, grad_gate[None], grad_up[None], grad_down[None])


def solution(mesh):
    sizes = dict(mesh.shape)
    fast = sizes["rep"] == 4 and sizes["exp"] == 8
    return jax.shard_map(
        on_quad if fast else on_device,
        mesh=mesh,
        in_specs=(
            P("exp", "rep"),
            P("exp", None),
            P("exp", None),
            P(),
            P(),
            P("exp", "rep"),
            P("exp", None, "rep"),
            P("exp", None, "rep"),
            P("exp", "rep", None),
        ),
        out_specs=(
            P("exp", "rep"),
            P("exp", "rep"),
            P("exp", None),
            P("exp", None, "rep"),
            P("exp", None, "rep"),
            P("exp", "rep", None),
        ),
        check_vma=False,
    )
```
